32 devices in a mesh: sec: 4 (over y, x), blk: 8 (over z, core).
Axes of the slice: x: 2, y: 2, z: 4, core: 2. Of those that a mesh axis runs over, the one named last changes fastest.
Arguments:
- tiles: bfloat16 [4, 8, 1024, 1024], P('sec', 'blk'), may hold values from -6 to 6
- row_taps: bfloat16 [4, 8, 9, 4, 512], P('sec', 'blk'), may hold values from -0.25 to 1
- col_taps: bfloat16 [4, 8, 9, 4, 512], P('sec', 'blk'), may hold values from -0.25 to 1
- row_starts: int32 [4, 8, 9, 512], P('sec', 'blk'), may hold values from 0 to 636, as said below
- col_starts: int32 [4, 8, 9, 512], P('sec', 'blk'), may hold values from 0 to 636, as said below
- feather_rows: bfloat16 [4, 8, 512], P('sec', 'blk'), may hold values from 0.19921875 to 1
- feather_cols: bfloat16 [4, 8, 512], P('sec', 'blk'), may hold values from 0.19921875 to 1
- footprint: int32 [4, 8, 9], P('sec', 'blk'), may hold values from 0 to 1, as said below
- offsets: int32 [4, 8, 9, 2], P('sec', 'blk'), may hold values from 0 to 384
Outputs:
- blended: bfloat16 [4, 8, 512, 512], P('sec', 'blk')
- level: bfloat16 [4, 8, 256, 256], P('sec', 'blk')
The draws below stay inside these ranges and needn't reach their ends.
Inputs may be any that keep to these rules, and one draw needn't show every extreme that they name: `footprint`: the centre slot (k = 4) is 1 for every block; a slot whose tile lies outside the grid of 2 by 4 positions is 0; the other slots are 0 or 1 independently. `row_starts`: output row 0 starts at 0 and output row 511 at 636; starts never exceed 640 - 4. `col_starts`: output column 0 starts at 0 and output column 511 at 636; starts never exceed 640 - 4.
All inputs are finite; a program needn't handle non-finite values.
Results may differ from the reference program's by a relative error of at most 0.0085.
Values may be sent and summed in bfloat16 or wider, within the bound.
No kernel may reach another device: no remote copies, remote signals or barrier semaphores. Data moves between devices by JAX's collectives and lax.ppermute only.
A program may use at most 128 MiB of HBM per device.

```python
import math
import jax
import jax.numpy as jnp
from jax import lax

TS = 1024
BS = 512
BAND = 640
TAPS = 4
GY = 4
SLOTS = 9
NSEC = 4
NPOS = 8


SLOT_PAIRS = [(-1, -1), (-1, 0), (-1, 1), (0, -1), (0, 0), (0, 1), (1, -1), (1, 0), (1, 1)]


def tap_positions(key):
    index = jnp.arange(BS, dtype=jnp.int32)
    base = index * (BAND - TAPS) // (BS - 1)
    jitter = jax.random.randint(key, (NSEC, NPOS, SLOTS, BS), -1, 2)
    inner = ((index > 0) & (index < BS - 1)).astype(jnp.int32)
    return jnp.clip(base[None, None, None, :] + jitter * inner[None, None, None, :], 0, BAND - TAPS).astype(jnp.int32)


def draw_row_starts(key, part):
    key = jax.random.fold_in(key, 11)
    return tap_positions(key)


def draw_col_starts(key, part):
    key = jax.random.fold_in(key, 13)
    return tap_positions(key)


def draw_footprint(key, part):
    key = jax.random.fold_in(key, 7)
    coins = jax.random.randint(key, (NSEC, NPOS, SLOTS), 0, 2)
    position = jnp.arange(NPOS, dtype=jnp.int32)
    grid_row = position // GY
    grid_col = position % GY
    columns = []
    for slot_index, pair in enumerate(SLOT_PAIRS):
        row_step, col_step = pair
        inside_rows = (grid_row + col_step >= 0) & (grid_row + col_step < NPOS // GY)
        inside_cols = (grid_col + row_step >= 0) & (grid_col + row_step < GY)
        inside = (inside_rows & inside_cols).astype(jnp.int32)
        if slot_index == 4:
            columns.append(jnp.ones((NSEC, NPOS), jnp.int32))
        else:
            columns.append(coins[:, :, slot_index] * inside[None, :])
    return jnp.stack(columns, -1).astype(jnp.int32)


def place_ends(result, key, smallest, top_value):
    shape = result.shape
    index_at = [jax.random.randint(jax.random.fold_in(key, axis), (), 0, shape[axis]) for axis in range(len(shape))]
    result = result.at[tuple(index_at)].set(smallest)
    longest = shape.index(max(shape))
    index_at[longest] = (index_at[longest] + 1) % shape[longest]
    return result.at[tuple(index_at)].set(top_value)


def block_scale(rng, dims, shards, least, top_value):
    gain = 1.0
    for dim, blocks in shards:
        steps = jax.random.uniform(jax.random.fold_in(jax.random.fold_in(rng, 6), dim), (blocks,), jnp.float32, least / len(shards), top_value / len(shards))
        gain = gain * jnp.repeat(jnp.exp(steps), dims[dim] // blocks).reshape((-1,) + (1,) * (len(dims) - 1 - dim))
    return gain


def scatter_about(rng, shape, deviation, most, cuts=(), kind=jnp.bfloat16):
    drawn = deviation * jax.random.normal(rng, shape, jnp.float32)
    if cuts:
        drawn = drawn * block_scale(rng, shape, cuts, -0.22, 0.18)
    return jnp.clip(drawn, -most, most).astype(kind)


def setup_inputs(seed: int = 0) -> dict:
    splits = jax.random.split(jax.random.key(seed), 10)
    tiles = scatter_about(splits[0], (NSEC, NPOS, TS, TS), 1.0, 6.0, ((0, 4), (1, 8)))
    row_taps = jnp.clip(-0.25 + 1.25 * jax.random.uniform(splits[1], (NSEC, NPOS, SLOTS, TAPS, BS), jnp.float32) ** block_scale(splits[1], (NSEC, NPOS, SLOTS, TAPS, BS), ((0, 4), (1, 8)), -0.2, 0.2), -0.25, 1.0).astype(jnp.bfloat16)
    col_taps = jnp.clip(-0.25 + 1.25 * jax.random.uniform(splits[2], (NSEC, NPOS, SLOTS, TAPS, BS), jnp.float32) ** block_scale(splits[2], (NSEC, NPOS, SLOTS, TAPS, BS), ((0, 4), (1, 8)), -0.2, 0.2), -0.25, 1.0).astype(jnp.bfloat16)
    row_starts = draw_row_starts(jax.random.fold_in(splits[9], 71), 0)
    col_starts = draw_col_starts(jax.random.fold_in(splits[9], 71), 0)
    feather_rows = jnp.clip(jnp.exp(math.log(1.0) - 1.6133518 * jax.random.uniform(splits[5], (NSEC, NPOS, BS), jnp.float32) ** block_scale(splits[5], (NSEC, NPOS, BS), ((0, 4), (1, 8)), -0.2, 0.2)), 0.19921875, 1.0).astype(jnp.bfloat16)
    feather_cols = jnp.clip(jnp.exp(math.log(1.0) - 1.6133518 * jax.random.uniform(splits[6], (NSEC, NPOS, BS), jnp.float32) ** block_scale(splits[6], (NSEC, NPOS, BS), ((0, 4), (1, 8)), -0.2, 0.2)), 0.19921875, 1.0).astype(jnp.bfloat16)
    footprint = draw_footprint(jax.random.fold_in(splits[9], 71), 0)
    offsets = place_ends(jax.random.randint(splits[8], (NSEC, NPOS, SLOTS, 2), 0, TS - BAND + 1), jax.random.fold_in(splits[8], 1), 0, TS - BAND).astype(jnp.int32)
    return {"tiles": tiles, "row_taps": row_taps, "col_taps": col_taps, "row_starts": row_starts, "col_starts": col_starts, "feather_rows": feather_rows, "feather_cols": feather_cols, "footprint": footprint, "offsets": offsets}


SLOT_PAIRS = [(-1, -1), (-1, 0), (-1, 1), (0, -1), (0, 0), (0, 1), (1, -1), (1, 0), (1, 1)]


def box_mean(field):
    total = field[..., 0::2, 0::2] + field[..., 1::2, 0::2] + field[..., 0::2, 1::2] + field[..., 1::2, 1::2]
    return total * 0.25


def resample(tile, corner, row_first, row_weight, col_first, col_weight):
    window = lax.dynamic_slice(tile, (corner[0].astype(jnp.int32), corner[1].astype(jnp.int32)), (BAND, BAND))
    rows = jnp.zeros((BS, BAND), jnp.float32)
    for tap in range(TAPS):
        picked = jnp.take(window, (row_first + tap).astype(jnp.int32), axis=0).astype(jnp.float32)
        rows = rows + row_weight[tap].astype(jnp.float32)[:, None] * picked
    rows = rows.astype(jnp.bfloat16)
    contrib = jnp.zeros((BS, BS), jnp.float32)
    for tap in range(TAPS):
        picked = jnp.take(rows, (col_first + tap).astype(jnp.int32), axis=1).astype(jnp.float32)
        contrib = contrib + col_weight[tap].astype(jnp.float32)[None, :] * picked
    return contrib.astype(jnp.bfloat16)


def render_section(section_tiles, section_rtaps, section_ctaps, section_rstart, section_cstart, section_fr, section_fc, section_foot, section_off):
    def render_block(position):
        numer = jnp.zeros((BS, BS), jnp.float32)
        denom = jnp.zeros((BS, BS), jnp.float32)
        block_rtaps = lax.dynamic_index_in_dim(section_rtaps, position, 0, keepdims=False)
        block_ctaps = lax.dynamic_index_in_dim(section_ctaps, position, 0, keepdims=False)
        block_rstart = lax.dynamic_index_in_dim(section_rstart, position, 0, keepdims=False)
        block_cstart = lax.dynamic_index_in_dim(section_cstart, position, 0, keepdims=False)
        block_off = lax.dynamic_index_in_dim(section_off, position, 0, keepdims=False)
        block_foot = lax.dynamic_index_in_dim(section_foot, position, 0, keepdims=False)
        for slot_index, pair in enumerate(SLOT_PAIRS):
            row_step, col_step = pair
            source = jnp.clip(position + col_step * GY + row_step, 0, NPOS - 1).astype(jnp.int32)
            tile = lax.dynamic_index_in_dim(section_tiles, source, 0, keepdims=False)
            prof_rows = lax.dynamic_index_in_dim(section_fr, source, 0, keepdims=False).astype(jnp.float32)
            prof_cols = lax.dynamic_index_in_dim(section_fc, source, 0, keepdims=False).astype(jnp.float32)
            contrib = resample(tile, block_off[slot_index], block_rstart[slot_index], block_rtaps[slot_index], block_cstart[slot_index], block_ctaps[slot_index])
            used = block_foot[slot_index]
            weight = used.astype(jnp.float32) * prof_rows[:, None] * prof_cols[None, :]
            numer = numer + weight * contrib.astype(jnp.float32)
            denom = denom + weight
        return (numer / denom).astype(jnp.bfloat16)

    return lax.map(render_block, jnp.arange(NPOS, dtype=jnp.int32))


def reference(tiles, row_taps, col_taps, row_starts, col_starts, feather_rows, feather_cols, footprint, offsets):
    blocks = []
    for section in range(NSEC):
        blocks.append(render_section(tiles[section], row_taps[section], col_taps[section], row_starts[section], col_starts[section], feather_rows[section], feather_cols[section], footprint[section], offsets[section]))
    blended = jnp.stack(blocks, 0)
    stacked = jnp.pad(blended.astype(jnp.float32), ((1, 1), (0, 0), (0, 0), (0, 0)))
    zsum = stacked[:-2] + 2.0 * stacked[1:-1] + stacked[2:]
    index = jnp.arange(NSEC)
    present = 4.0 - (index == 0).astype(jnp.float32) - (index == NSEC - 1).astype(jnp.float32)
    smooth = zsum / present[:, None, None, None]
    level = box_mean(smooth).astype(jnp.bfloat16)
    return blended, level
```

```python
import functools

import jax
import jax.numpy as jnp
from jax import lax
from jax.experimental import pallas as pl
from jax.experimental.pallas import tpu as pltpu
from jax.sharding import PartitionSpec as P

BAND = 640
GY = 4
TAPS = 4
LANE = 128
WIN = BAND + LANE
EXTRA = 16
VMEM_LIMIT = 40 * 1024 * 1024

bf16 = jnp.bfloat16
f32 = jnp.float32


def vmem():
    return pl.BlockSpec(memory_space=pltpu.VMEM)


def smem():
    return pl.BlockSpec(memory_space=pltpu.SMEM)


def hbm():
    return pl.BlockSpec(memory_space=pltpu.HBM)


def params():
    return pltpu.CompilerParams(vmem_limit_bytes=VMEM_LIMIT)


def cost(flops, nbytes):
    return pl.CostEstimate(flops=int(flops), bytes_accessed=int(nbytes), transcendentals=0)


def slot_of(column, role, step):
    odd = column % 2
    if role == 0:
        across = 0
    elif role == 1:
        across = 1 - 2 * odd
    else:
        across = 2 * odd - 1
    return 3 * (across + 1) + (step + 1)


def my_column():
    return lax.rem(lax.axis_index("blk"), GY)


def my_row():
    return lax.div(lax.axis_index("blk"), GY)


def step_of(move):
    if move == "swap":
        return 1 - 2 * my_row()
    return -move


def pack_kernel(moves, rt_ref, ct_ref, rs_ref, cs_ref, foot_ref, off_ref, fr_ref, fc_ref, tile_ref, *refs):
    outs, (buf, fbuf, sems) = refs[:-3], refs[-3:]
    ext_ref, packed = outs[0], outs[1:]
    size = tile_ref.shape[0]
    whole = pltpu.make_async_copy(tile_ref, ext_ref.at[pl.ds(0, size)], sems.at[0])
    whole.start()
    edge = fr_ref.shape[1]
    fbuf[...] = jnp.zeros(fbuf.shape, bf16)
    fbuf[0:1, 0:edge] = fr_ref[...]
    fbuf[0:1, edge : 2 * edge] = fc_ref[...]
    tail = pltpu.make_async_copy(fbuf, ext_ref.at[pl.ds(size, EXTRA)], sems.at[1])
    tail.start()
    column = my_column()
    most = (size - BAND) // LANE - 1
    steps = [0] + [step_of(move) for move in moves]
    for group, step in enumerate(steps):
        for role in range(3):
            k = jnp.clip(slot_of(column, role, step), 0, 8)
            used = foot_ref[k].astype(f32)
            buf[0:TAPS] = rt_ref[k].astype(f32)
            buf[TAPS : 2 * TAPS] = ct_ref[k].astype(f32) * used
            for dim, ref in enumerate((rs_ref, cs_ref)):
                off = off_ref[2 * k + dim]
                base = jnp.minimum(lax.div(off, LANE), most)
                rel = ref[pl.ds(k, 1), :] + (off - base * LANE)
                high = lax.shift_right_logical(rel, 5)
                buf[8 + 2 * dim : 9 + 2 * dim] = high.astype(f32)
                buf[9 + 2 * dim : 10 + 2 * dim] = (rel - high * 32).astype(f32)
                buf[12 + dim : 13 + dim] = jnp.zeros((1, edge), f32) + base.astype(f32)
            buf[14:16] = jnp.zeros((2, edge), f32)
            packed[group][role] = buf[...].astype(bf16)
    whole.wait()
    tail.wait()


def pack(moves, rt, ct, rs, cs, foot, off, fr, fc, tile):
    size, edge = tile.shape[0], rs.shape[1]
    groups = 1 + len(moves)
    return pl.pallas_call(
        functools.partial(pack_kernel, moves),
        name="pack",
        out_shape=[jax.ShapeDtypeStruct((size + EXTRA, tile.shape[1]), bf16)]
        + [jax.ShapeDtypeStruct((3, 16, edge), bf16)] * groups,
        in_specs=[vmem()] * 4 + [smem()] * 2 + [vmem()] * 2 + [hbm()],
        out_specs=[hbm()] + [vmem()] * groups,
        scratch_shapes=[
            pltpu.VMEM((16, edge), f32),
            pltpu.VMEM((EXTRA, tile.shape[1]), bf16),
            pltpu.SemaphoreType.DMA((2,)),
        ],
        compiler_params=params(),
        cost_estimate=cost(1e6, 5e6),
    )(rt, ct, rs, cs, foot, off, fr, fc, tile)


def row_matrix(prm, edge):
    cols = prm.T
    rel = cols[:, 8:9] * 32.0 + cols[:, 9:10]
    rel = jnp.broadcast_to(rel, (edge, LANE))
    taps = [jnp.broadcast_to(cols[:, q : q + 1], (edge, LANE)).astype(bf16) for q in range(TAPS)]
    lane = lax.broadcasted_iota(jnp.int32, (edge, LANE), 1).astype(f32)
    parts = []
    for h in range(WIN // LANE):
        place = ((lane + float(LANE * h)) - rel).astype(bf16)
        part = jnp.zeros((edge, LANE), bf16)
        for q in range(TAPS):
            part = jnp.where(place == bf16(q), taps[q], part)
        parts.append(part)
    return jnp.concatenate(parts, axis=1)


def col_matrix(prm, edge):
    rel = prm[10:11] * 32.0 + prm[11:12]
    taps = [jnp.broadcast_to(prm[TAPS + q : TAPS + q + 1], (LANE, edge)).astype(bf16) for q in range(TAPS)]
    sub = lax.broadcasted_iota(jnp.int32, (LANE, edge), 0).astype(f32)
    parts = []
    for h in range(WIN // LANE):
        place = (sub - (rel - float(LANE * h))).astype(bf16)
        part = jnp.zeros((LANE, edge), bf16)
        for q in range(TAPS):
            part = jnp.where(place == bf16(q), taps[q], part)
        parts.append(part)
    return jnp.concatenate(parts, axis=0)


def contrib_kernel(slots, only_middle, feather_row, prm_ref, *refs):
    count = len(slots)
    tiles, out_ref = refs[:count], refs[count]
    win, fth, sems = refs[count + 1 :]
    edge = out_ref.shape[1]
    size = tiles[0].shape[0] - EXTRA

    def work():
        copies = []
        for s, slot in enumerate(slots):
            base = prm_ref[slot].astype(f32)
            r0 = pl.multiple_of(jnp.max(base[12:13, 0:LANE]).astype(jnp.int32) * LANE, LANE)
            c0 = pl.multiple_of(jnp.max(base[13:14, 0:LANE]).astype(jnp.int32) * LANE, LANE)
            window = pltpu.make_async_copy(
                tiles[s].at[pl.ds(r0, WIN), pl.ds(c0, WIN)], win.at[s], sems.at[s, 0]
            )
            feather = pltpu.make_async_copy(tiles[s].at[pl.ds(size, EXTRA)], fth.at[s], sems.at[s, 1])
            window.start()
            feather.start()
            copies.append((window, feather))
        total = None
        profiles = []
        for s, slot in enumerate(slots):
            prm = prm_ref[slot].astype(f32)
            rmat = row_matrix(prm, edge)
            cmat = col_matrix(prm, edge)
            copies[s][0].wait()
            copies[s][1].wait()
            rows = jnp.dot(rmat, win[s], preferred_element_type=f32).astype(bf16)
            contrib = jnp.dot(rows, cmat, preferred_element_type=f32)
            profile = fth[s].astype(f32)
            profiles += [profile[0:1, :edge], profile[0:1, edge:]]
            contrib = contrib * profile[:, :edge].T[:, 0:1] * profile[0:1, edge:]
            total = contrib if total is None else total + contrib
        out_ref[0:edge] = total.astype(out_ref.dtype)
        before = [jnp.zeros((feather_row, edge), f32)] if feather_row else []
        after = [jnp.zeros((EXTRA - feather_row - len(profiles), edge), f32)]
        out_ref[edge:] = jnp.concatenate(before + profiles + after, axis=0).astype(out_ref.dtype)

    if only_middle:
        column = my_column()
        pl.when(jnp.logical_and(column > 0, column < GY - 1))(work)
    else:
        work()


def contributions(name, prm, slots, tiles, edge, only_middle=False, feather_row=0):
    count = len(slots)
    return pl.pallas_call(
        functools.partial(contrib_kernel, slots, only_middle, feather_row),
        name=name,
        out_shape=jax.ShapeDtypeStruct((edge + EXTRA, edge), bf16),
        in_specs=[vmem()] + [hbm()] * count,
        out_specs=vmem(),
        scratch_shapes=[
            pltpu.VMEM((count, WIN, WIN), bf16),
            pltpu.VMEM((count, EXTRA, tiles[0].shape[1]), bf16),
            pltpu.SemaphoreType.DMA((count, 2)),
        ],
        compiler_params=params(),
        cost_estimate=cost(1.0e9 * count * 2, 1.2e6 * count + 5e5),
    )(prm, *tiles)


def weights_of(foot_ref, column, step, rows, roles):
    total = None
    cols = rows.T
    for role in roles:
        slot = slot_of(column, role, step)
        inside = jnp.logical_and(slot >= 0, slot < 9)
        used = jnp.where(inside, foot_ref[jnp.clip(slot, 0, 8)], 0).astype(f32)
        term = cols[:, 2 * role : 2 * role + 1] * (rows[2 * role + 1 : 2 * role + 2] * used)
        total = term if total is None else total + term
    return total


def same_row_kernel(foot_ref, own_ref, cross_ref, numer_ref, denom_ref):
    edge = own_ref.shape[1]
    rows = own_ref[edge:].astype(f32) + cross_ref[edge:].astype(f32)
    numer_ref[...] = own_ref[0:edge].astype(f32) + cross_ref[0:edge].astype(f32)
    denom_ref[...] = weights_of(foot_ref, my_column(), 0, rows, range(3))


def same_row(foot, own, cross, edge):
    return pl.pallas_call(
        same_row_kernel,
        name="same_row",
        out_shape=[jax.ShapeDtypeStruct((edge, edge), f32)] * 2,
        in_specs=[smem(), vmem(), vmem()],
        out_specs=[vmem(), vmem()],
        compiler_params=params(),
        cost_estimate=cost(4e6, 3e6),
    )(foot, own, cross)


def finish_kernel(moves, foot_ref, numer_ref, denom_ref, *refs):
    arrived, (blended_ref, pooled_ref, half) = refs[:-3], refs[-3:]
    edge = numer_ref.shape[0]
    numer, denom = numer_ref[...], denom_ref[...]
    for n, move in enumerate(moves):
        first, second = arrived[2 * n], arrived[2 * n + 1]
        numer = numer + (first[0:edge].astype(f32) + second[0:edge].astype(f32))
        rows = first[edge:].astype(f32) + second[edge:].astype(f32)
        denom = denom + weights_of(foot_ref, my_column(), step_of(move), rows, range(3))
    blended = (numer / denom).astype(bf16)
    blended_ref[...] = blended
    source = lax.broadcasted_iota(jnp.int32, (edge, edge // 2), 0)
    target = lax.broadcasted_iota(jnp.int32, (edge, edge // 2), 1)
    pairs = jnp.where(lax.shift_right_logical(source, 1) == target, 1.0, 0.0).astype(bf16)
    pooled = jnp.dot(blended, pairs, preferred_element_type=f32) * 0.25
    for h in range(edge // 2 // LANE):
        half[h] = pooled[:, h * LANE : (h + 1) * LANE]
        total = half[h, pl.ds(0, edge // 2, stride=2), :] + half[h, pl.ds(1, edge // 2, stride=2), :]
        pooled_ref[:, h * LANE : (h + 1) * LANE] = total.astype(bf16)


def finish(moves, foot, numer, denom, arrived, edge):
    return pl.pallas_call(
        functools.partial(finish_kernel, moves),
        name="finish",
        out_shape=[
            jax.ShapeDtypeStruct((edge, edge), bf16),
            jax.ShapeDtypeStruct((edge // 2, edge // 2), bf16),
        ],
        in_specs=[smem(), vmem(), vmem()] + [vmem()] * len(arrived),
        out_specs=[vmem(), vmem()],
        scratch_shapes=[pltpu.VMEM((edge // 2 // LANE, edge, LANE), f32)],
        compiler_params=params(),
        cost_estimate=cost(3e8, 4e6),
    )(foot, numer, denom, *arrived)


def per_device(
    tiles, row_taps, col_taps, row_starts, col_starts, feather_rows, feather_cols, footprint, offsets
):
    tile = tiles[0, 0]
    edge = row_starts.shape[3]
    devices = lax.axis_size("blk")
    rows = devices // GY
    moves = ["swap"] if rows == 2 else [1, -1]
    foot = footprint.reshape(9)

    def along(move, value, columns=range(GY), back=False):
        pairs = []
        for r in range(rows):
            to = (1 - r) if move == "swap" else r + (-move if back else move)
            if 0 <= to < rows:
                pairs += [(r * GY + c, to * GY + c) for c in columns]
        return lax.ppermute(value, "blk", pairs)

    def mate(value):
        return lax.ppermute(value, "blk", [(i, i ^ 1) for i in range(devices)])

    def cross(value):
        pairs = []
        for r in range(rows):
            for c in range(1, GY - 1, 2):
                pairs += [(r * GY + c, r * GY + c + 1), (r * GY + c + 1, r * GY + c)]
        return lax.ppermute(value, "blk", pairs)

    packed = pack(
        moves,
        row_taps[0, 0],
        col_taps[0, 0],
        row_starts[0, 0],
        col_starts[0, 0],
        foot,
        offsets.reshape(18),
        feather_rows[0],
        feather_cols[0],
        tile,
    )
    ext, own_prm, move_prm = packed[0], packed[1], packed[2:]
    ext_mate = mate(ext)
    asked = [along(move, prm, back=True) for move, prm in zip(moves, move_prm)]
    cross_prm = cross(jnp.stack([own_prm[2]] + [prm[2] for prm in asked]))
    arrived = []
    for n, move in enumerate(moves):
        over = contributions("cross_sum", cross_prm, [1 + n], [ext], edge, True, 4)
        over = cross(over)
        local = contributions("local_sum", asked[n], [0, 1], [ext, ext_mate], edge)
        arrived.append(along(move, local, [0, GY - 1]))
        arrived.append(along(move, local + over, range(1, GY - 1)))
    side = cross(contributions("cross_own", cross_prm, [0], [ext], edge, True, 4))
    own = contributions("local_own", own_prm, [0, 1], [ext, ext_mate], edge)
    numer, denom = same_row(foot, own, side, edge)
    blended, pooled = finish(moves, foot, numer, denom, arrived, edge)
    sections = lax.axis_size("sec")
    before = lax.ppermute(pooled, "sec", [(i, i + 1) for i in range(sections - 1)])
    after = lax.ppermute(pooled, "sec", [(i + 1, i) for i in range(sections - 1)])
    index = lax.axis_index("sec")
    present = 4.0 - (index == 0).astype(f32) - (index == sections - 1).astype(f32)
    level = (before.astype(f32) + 2.0 * pooled.astype(f32) + after.astype(f32)) / present
    return blended[None, None], level.astype(bf16)[None, None]


def solution(mesh):
    return jax.shard_map(
        per_device,
        mesh=mesh,
        in_specs=(
            P("sec", "blk", None, None),
            P("sec", "blk", None, None, None),
            P("sec", "blk", None, None, None),
            P("sec", "blk", None, None),
            P("sec", "blk", None, None),
            P("sec", "blk", None),
            P("sec", "blk", None),
            P("sec", "blk", None),
            P("sec", "blk", None, None),
        ),
        out_specs=(P("sec", "blk", None, None), P("sec", "blk", None, None)),
        check_vma=False,
    )
```

```python
import functools

import jax
import jax.numpy as jnp
from jax import lax
from jax.experimental import pallas as pl
from jax.experimental.pallas import tpu as pltpu
from jax.sharding import PartitionSpec as P

BAND = 640
GY = 4
TAPS = 4
LANE = 128
WIN = BAND + LANE
EXTRA = 16
VMEM_LIMIT = 40 * 1024 * 1024

bf16 = jnp.bfloat16
f32 = jnp.float32


def vmem():
    return pl.BlockSpec(memory_space=pltpu.VMEM)


def smem():
    return pl.BlockSpec(memory_space=pltpu.SMEM)


def hbm():
    return pl.BlockSpec(memory_space=pltpu.HBM)


def params():
    return pltpu.CompilerParams(vmem_limit_bytes=VMEM_LIMIT)


def cost(flops, nbytes):
    return pl.CostEstimate(flops=int(flops), bytes_accessed=int(nbytes), transcendentals=0)


def slot_of(column, role, step):
    odd = column % 2
    if role == 0:
        across = 0
    elif role == 1:
        across = 1 - 2 * odd
    else:
        across = 2 * odd - 1
    return 3 * (across + 1) + (step + 1)


def my_column():
    return lax.rem(lax.axis_index("blk"), GY)


def my_row():
    return lax.div(lax.axis_index("blk"), GY)


def step_of(move):
    if move == "swap":
        return 1 - 2 * my_row()
    return -move


def pack_kernel(moves, rt_ref, ct_ref, rs_ref, cs_ref, foot_ref, off_ref, fr_ref, fc_ref, tile_ref, *refs):
    outs, (buf, fbuf, sems) = refs[:-3], refs[-3:]
    ext_ref, packed = outs[0], outs[1:]
    size = tile_ref.shape[0]
    whole = pltpu.make_async_copy(tile_ref, ext_ref.at[pl.ds(0, size)], sems.at[0])
    whole.start()
    edge = fr_ref.shape[1]
    fbuf[...] = jnp.zeros(fbuf.shape, bf16)
    fbuf[0:1, 0:edge] = fr_ref[...]
    fbuf[0:1, edge : 2 * edge] = fc_ref[...]
    tail = pltpu.make_async_copy(fbuf, ext_ref.at[pl.ds(size, EXTRA)], sems.at[1])
    tail.start()
    column = my_column()
    most = (size - BAND) // LANE - 1
    steps = [0] + [step_of(move) for move in moves]
    for group, step in enumerate(steps):
        for role in range(3):
            k = jnp.clip(slot_of(column, role, step), 0, 8)
            used = foot_ref[k].astype(f32)
            buf[0:TAPS] = rt_ref[k].astype(f32)
            buf[TAPS : 2 * TAPS] = ct_ref[k].astype(f32) * used
            for dim, ref in enumerate((rs_ref, cs_ref)):
                off = off_ref[2 * k + dim]
                base = jnp.minimum(lax.div(off, LANE), most)
                rel = ref[pl.ds(k, 1), :] + (off - base * LANE)
                high = lax.shift_right_logical(rel, 5)
                buf[8 + 2 * dim : 9 + 2 * dim] = high.astype(f32)
                buf[9 + 2 * dim : 10 + 2 * dim] = (rel - high * 32).astype(f32)
                buf[12 + dim : 13 + dim] = jnp.zeros((1, edge), f32) + base.astype(f32)
            buf[14:16] = jnp.zeros((2, edge), f32)
            packed[group][role] = buf[...].astype(bf16)
    whole.wait()
    tail.wait()


def pack(moves, rt, ct, rs, cs, foot, off, fr, fc, tile):
    size, edge = tile.shape[0], rs.shape[1]
    groups = 1 + len(moves)
    return pl.pallas_call(
        functools.partial(pack_kernel, moves),
        name="pack",
        out_shape=[jax.ShapeDtypeStruct((size + EXTRA, tile.shape[1]), bf16)]
        + [jax.ShapeDtypeStruct((3, 16, edge), bf16)] * groups,
        in_specs=[vmem()] * 4 + [smem()] * 2 + [vmem()] * 2 + [hbm()],
        out_specs=[hbm()] + [vmem()] * groups,
        scratch_shapes=[
            pltpu.VMEM((16, edge), f32),
            pltpu.VMEM((EXTRA, tile.shape[1]), bf16),
            pltpu.SemaphoreType.DMA((2,)),
        ],
        compiler_params=params(),
        cost_estimate=cost(1e6, 5e6),
    )(rt, ct, rs, cs, foot, off, fr, fc, tile)


def row_matrix(prm, edge):
    cols = prm.T
    rel = cols[:, 8:9] * 32.0 + cols[:, 9:10]
    rel = jnp.broadcast_to(rel, (edge, LANE))
    taps = [jnp.broadcast_to(cols[:, q : q + 1], (edge, LANE)).astype(bf16) for q in range(TAPS)]
    lane = lax.broadcasted_iota(jnp.int32, (edge, LANE), 1).astype(f32)
    parts = []
    for h in range(WIN // LANE):
        place = ((lane + float(LANE * h)) - rel).astype(bf16)
        part = jnp.zeros((edge, LANE), bf16)
        for q in range(TAPS):
            part = jnp.where(place == bf16(q), taps[q], part)
        parts.append(part)
    return jnp.concatenate(parts, axis=1)


def col_matrix(prm, edge):
    rel = prm[10:11] * 32.0 + prm[11:12]
    taps = [jnp.broadcast_to(prm[TAPS + q : TAPS + q + 1], (LANE, edge)).astype(bf16) for q in range(TAPS)]
    sub = lax.broadcasted_iota(jnp.int32, (LANE, edge), 0).astype(f32)
    parts = []
    for h in range(WIN // LANE):
        place = (sub - (rel - float(LANE * h))).astype(bf16)
        part = jnp.zeros((LANE, edge), bf16)
        for q in range(TAPS):
            part = jnp.where(place == bf16(q), taps[q], part)
        parts.append(part)
    return jnp.concatenate(parts, axis=0)


def contrib_kernel(slots, only_middle, feather_row, prm_ref, *refs):
    count = len(slots)
    tiles, out_ref = refs[:count], refs[count]
    win, fth, sems = refs[count + 1 :]
    edge = out_ref.shape[1]
    size = tiles[0].shape[0] - EXTRA

    def work():
        copies = []
        for s, slot in enumerate(slots):
            base = prm_ref[slot].astype(f32)
            r0 = pl.multiple_of(jnp.max(base[12:13, 0:LANE]).astype(jnp.int32) * LANE, LANE)
            c0 = pl.multiple_of(jnp.max(base[13:14, 0:LANE]).astype(jnp.int32) * LANE, LANE)
            window = pltpu.make_async_copy(
                tiles[s].at[pl.ds(r0, WIN), pl.ds(c0, WIN)], win.at[s], sems.at[s, 0]
            )
            feather = pltpu.make_async_copy(tiles[s].at[pl.ds(size, EXTRA)], fth.at[s], sems.at[s, 1])
            window.start()
            feather.start()
            copies.append((window, feather))
        total = None
        profiles = []
        for s, slot in enumerate(slots):
            prm = prm_ref[slot].astype(f32)
            rmat = row_matrix(prm, edge)
            cmat = col_matrix(prm, edge)
            copies[s][0].wait()
            copies[s][1].wait()
            rows = jnp.dot(rmat, win[s], preferred_element_type=f32).astype(bf16)
            contrib = jnp.dot(rows, cmat, preferred_element_type=f32)
            profile = fth[s].astype(f32)
            profiles += [profile[0:1, :edge], profile[0:1, edge:]]
            contrib = contrib * profile[:, :edge].T[:, 0:1] * profile[0:1, edge:]
            total = contrib if total is None else total + contrib
        out_ref[0:edge] = total.astype(out_ref.dtype)
        before = [jnp.zeros((feather_row, edge), f32)] if feather_row else []
        after = [jnp.zeros((EXTRA - feather_row - len(profiles), edge), f32)]
        out_ref[edge:] = jnp.concatenate(before + profiles + after, axis=0).astype(out_ref.dtype)

    if only_middle:
        column = my_column()
        pl.when(jnp.logical_and(column > 0, column < GY - 1))(work)
    else:
        work()


def contributions(name, prm, slots, tiles, edge, only_middle=False, feather_row=0):
    count = len(slots)
    return pl.pallas_call(
        functools.partial(contrib_kernel, slots, only_middle, feather_row),
        name=name,
        out_shape=jax.ShapeDtypeStruct((edge + EXTRA, edge), bf16),
        in_specs=[vmem()] + [hbm()] * count,
        out_specs=vmem(),
        scratch_shapes=[
            pltpu.VMEM((count, WIN, WIN), bf16),
            pltpu.VMEM((count, EXTRA, tiles[0].shape[1]), bf16),
            pltpu.SemaphoreType.DMA((count, 2)),
        ],
        compiler_params=params(),
        cost_estimate=cost(1.0e9 * count * 2, 1.2e6 * count + 5e5),
    )(prm, *tiles)


def weights_of(foot_ref, column, step, rows, roles):
    total = None
    cols = rows.T
    for role in roles:
        slot = slot_of(column, role, step)
        inside = jnp.logical_and(slot >= 0, slot < 9)
        used = jnp.where(inside, foot_ref[jnp.clip(slot, 0, 8)], 0).astype(f32)
        term = cols[:, 2 * role : 2 * role + 1] * (rows[2 * role + 1 : 2 * role + 2] * used)
        total = term if total is None else total + term
    return total


def same_row_kernel(foot_ref, own_ref, cross_ref, numer_ref, denom_ref):
    edge = own_ref.shape[1]
    rows = own_ref[edge:].astype(f32) + cross_ref[edge:].astype(f32)
    numer_ref[...] = own_ref[0:edge].astype(f32) + cross_ref[0:edge].astype(f32)
    denom_ref[...] = weights_of(foot_ref, my_column(), 0, rows, range(3))


def same_row(foot, own, cross, edge):
    return pl.pallas_call(
        same_row_kernel,
        name="same_row",
        out_shape=[jax.ShapeDtypeStruct((edge, edge), f32)] * 2,
        in_specs=[smem(), vmem(), vmem()],
        out_specs=[vmem(), vmem()],
        compiler_params=params(),
        cost_estimate=cost(4e6, 3e6),
    )(foot, own, cross)


def finish_kernel(moves, foot_ref, numer_ref, denom_ref, *refs):
    arrived, (blended_ref, pooled_ref, half) = refs[:-3], refs[-3:]
    edge = numer_ref.shape[0]
    numer, denom = numer_ref[...], denom_ref[...]
    for n, move in enumerate(moves):
        first, second = arrived[2 * n], arrived[2 * n + 1]
        numer = numer + (first[0:edge].astype(f32) + second[0:edge].astype(f32))
        rows = first[edge:].astype(f32) + second[edge:].astype(f32)
        denom = denom + weights_of(foot_ref, my_column(), step_of(move), rows, range(3))
    blended = (numer / denom).astype(bf16)
    blended_ref[...] = blended
    source = lax.broadcasted_iota(jnp.int32, (edge, edge // 2), 0)
    target = lax.broadcasted_iota(jnp.int32, (edge, edge // 2), 1)
    pairs = jnp.where(lax.shift_right_logical(source, 1) == target, 1.0, 0.0).astype(bf16)
    pooled = jnp.dot(blended, pairs, preferred_element_type=f32) * 0.25
    for h in range(edge // 2 // LANE):
        half[h] = pooled[:, h * LANE : (h + 1) * LANE]
        total = half[h, pl.ds(0, edge // 2, stride=2), :] + half[h, pl.ds(1, edge // 2, stride=2), :]
        pooled_ref[:, h * LANE : (h + 1) * LANE] = total.astype(bf16)


def finish(moves, foot, numer, denom, arrived, edge):
    return pl.pallas_call(
        functools.partial(finish_kernel, moves),
        name="finish",
        out_shape=[
            jax.ShapeDtypeStruct((edge, edge), bf16),
            jax.ShapeDtypeStruct((edge // 2, edge // 2), bf16),
        ],
        in_specs=[smem(), vmem(), vmem()] + [vmem()] * len(arrived),
        out_specs=[vmem(), vmem()],
        scratch_shapes=[pltpu.VMEM((edge // 2 // LANE, edge, LANE), f32)],
        compiler_params=params(),
        cost_estimate=cost(3e8, 4e6),
    )(foot, numer, denom, *arrived)


def general_device(
    tiles, row_taps, col_taps, row_starts, col_starts, feather_rows, feather_cols, footprint, offsets
):
    tile = tiles[0, 0]
    edge = row_starts.shape[3]
    devices = lax.axis_size("blk")
    rows = devices // GY
    moves = ["swap"] if rows == 2 else [1, -1]
    foot = footprint.reshape(9)

    def along(move, value, columns=range(GY), back=False):
        pairs = []
        for r in range(rows):
            to = (1 - r) if move == "swap" else r + (-move if back else move)
            if 0 <= to < rows:
                pairs += [(r * GY + c, to * GY + c) for c in columns]
        return lax.ppermute(value, "blk", pairs)

    def mate(value):
        return lax.ppermute(value, "blk", [(i, i ^ 1) for i in range(devices)])

    def cross(value):
        pairs = []
        for r in range(rows):
            for c in range(1, GY - 1, 2):
                pairs += [(r * GY + c, r * GY + c + 1), (r * GY + c + 1, r * GY + c)]
        return lax.ppermute(value, "blk", pairs)

    packed = pack(
        moves,
        row_taps[0, 0],
        col_taps[0, 0],
        row_starts[0, 0],
        col_starts[0, 0],
        foot,
        offsets.reshape(18),
        feather_rows[0],
        feather_cols[0],
        tile,
    )
    ext, own_prm, move_prm = packed[0], packed[1], packed[2:]
    ext_mate = mate(ext)
    asked = [along(move, prm, back=True) for move, prm in zip(moves, move_prm)]
    cross_prm = cross(jnp.stack([own_prm[2]] + [prm[2] for prm in asked]))
    arrived = []
    for n, move in enumerate(moves):
        over = contributions("cross_sum", cross_prm, [1 + n], [ext], edge, True, 4)
        over = cross(over)
        local = contributions("local_sum", asked[n], [0, 1], [ext, ext_mate], edge)
        arrived.append(along(move, local, [0, GY - 1]))
        arrived.append(along(move, local + over, range(1, GY - 1)))
    side = cross(contributions("cross_own", cross_prm, [0], [ext], edge, True, 4))
    own = contributions("local_own", own_prm, [0, 1], [ext, ext_mate], edge)
    numer, denom = same_row(foot, own, side, edge)
    blended, pooled = finish(moves, foot, numer, denom, arrived, edge)
    sections = lax.axis_size("sec")
    before = lax.ppermute(pooled, "sec", [(i, i + 1) for i in range(sections - 1)])
    after = lax.ppermute(pooled, "sec", [(i + 1, i) for i in range(sections - 1)])
    index = lax.axis_index("sec")
    present = 4.0 - (index == 0).astype(f32) - (index == sections - 1).astype(f32)
    level = (before.astype(f32) + 2.0 * pooled.astype(f32) + after.astype(f32)) / present
    return blended[None, None], level.astype(bf16)[None, None]


HALF = 12
PROFILE = 24
BESIDE = 26
SCALARS = 28
CORNER = 8
ROWS = 32
TILE = 1024
PREPARE_VMEM = 40 * 1024 * 1024
WORK_VMEM = 40 * 1024 * 1024


def is_outer():
    column = my_column()
    return jnp.logical_or(column == 0, column == GY - 1)


def prepare_kernel(rt_hbm, ct_hbm, rs_hbm, cs_hbm, foot_hbm, off_hbm, fr_hbm, fc_hbm, *refs):
    outs = refs[:4]
    rt_ref, ct_ref, rs_ref, cs_ref, fr_ref, fc_ref, foot_ref, off_ref, buf, sems = refs[4:]
    pairs = [
        (off_hbm, off_ref),
        (foot_hbm, foot_ref),
        (rt_hbm, rt_ref),
        (ct_hbm, ct_ref),
        (rs_hbm, rs_ref),
        (cs_hbm, cs_ref),
        (fr_hbm, fr_ref),
        (fc_hbm, fc_ref),
    ]
    copies = [pltpu.make_async_copy(a, b, sems.at[i]) for i, (a, b) in enumerate(pairs)]
    for copy in copies:
        copy.start()
    for copy in copies:
        copy.wait()
    edge = fr_ref.shape[1]
    column = my_column()
    over = 1 - 2 * my_row()
    most = (TILE - BAND) // LANE - 1
    lane = lax.broadcasted_iota(jnp.int32, (1, edge), 1)
    scalars = jnp.zeros((1, edge), f32)
    for n in range(6):
        slot = slot_of(column, n % 3, 0 if n < 3 else over)
        inside = jnp.logical_and(slot >= 0, slot < 9)
        used = jnp.where(inside, foot_ref[0, jnp.clip(slot, 0, 8)], 0).astype(f32)
        scalars = jnp.where(lane == n, used, scalars)

    def message(out_ref, slots, profile_row):
        row = scalars
        buf[...] = jnp.zeros(buf.shape, f32)
        for half, (role, step) in enumerate(slots):
            k = jnp.clip(slot_of(column, role, step), 0, 8)
            used = foot_ref[0, k].astype(f32)
            at = half * HALF
            buf[at : at + TAPS] = rt_ref[k].astype(f32)
            buf[at + TAPS : at + 2 * TAPS] = ct_ref[k].astype(f32) * used
            for dim, ref in enumerate((rs_ref, cs_ref)):
                off = off_ref[dim, k]
                base = jnp.minimum(lax.div(off, LANE), most)
                rel = ref[k] + (off - base * LANE)
                high = lax.shift_right_logical(rel, 5)
                first = at + 2 * TAPS + 2 * dim
                buf[first : first + 1] = high.astype(f32)
                buf[first + 1 : first + 2] = (rel - high * 32).astype(f32)
                row = jnp.where(lane == CORNER + 2 * half + dim, base.astype(f32), row)
        buf[profile_row : profile_row + 1] = fr_ref[...].astype(f32)
        buf[profile_row + 1 : profile_row + 2] = fc_ref[...].astype(f32)
        buf[SCALARS : SCALARS + 1] = row
        out_ref[...] = buf[...].astype(bf16)

    message(outs[0], [(0, over), (1, over)], PROFILE)
    message(outs[1], [(2, over)], PROFILE)
    message(outs[2], [(2, 0)], BESIDE)
    message(outs[3], [(0, 0), (1, 0)], PROFILE)


def prepare(rt, ct, rs, cs, foot, off, fr, fc):
    edge = fr.shape[1]
    args = [pltpu.with_memory_space_constraint(x, pltpu.HBM) for x in (rt, ct, rs, cs, foot, off, fr, fc)]
    return pl.pallas_call(
        prepare_kernel,
        name="prepare",
        out_shape=[jax.ShapeDtypeStruct((ROWS, edge), bf16)] * 4,
        in_specs=[hbm()] * 8,
        out_specs=[vmem()] * 4,
        scratch_shapes=[pltpu.VMEM(x.shape, x.dtype) for x in (rt, ct, rs, cs, fr, fc)]
        + [pltpu.SMEM(x.shape, x.dtype) for x in (foot, off)]
        + [pltpu.VMEM((ROWS, edge), f32), pltpu.SemaphoreType.DMA((8,))],
        compiler_params=pltpu.CompilerParams(vmem_limit_bytes=PREPARE_VMEM),
        cost_estimate=cost(1e6, 2e5),
    )(*args)


def fetch_kernel(tile_ref, out_ref, sems):
    parts = sems.shape[0]
    size = out_ref.shape[0] // parts
    copies = [
        pltpu.make_async_copy(tile_ref.at[pl.ds(n * size, size)], out_ref.at[pl.ds(n * size, size)], sems.at[n])
        for n in range(parts)
    ]
    for copy in copies:
        copy.start()
    for copy in copies:
        copy.wait()


def fetch(tile):
    return pl.pallas_call(
        fetch_kernel,
        name="fetch",
        out_shape=pltpu.VMEM(tile.shape, tile.dtype),
        in_specs=[hbm()],
        out_specs=vmem(),
        scratch_shapes=[pltpu.SemaphoreType.DMA((8,))],
        compiler_params=pltpu.CompilerParams(vmem_limit_bytes=PREPARE_VMEM),
        cost_estimate=cost(1e6, 4e6),
    )(pltpu.with_memory_space_constraint(tile, pltpu.HBM))


def scalar_of(msg, n):
    lane = lax.broadcasted_iota(jnp.int32, (1, LANE), 1)
    return jnp.sum(jnp.where(lane == n, msg[SCALARS : SCALARS + 1, 0:LANE], 0.0))


def corner(msg, half):
    r0 = pl.multiple_of(scalar_of(msg, CORNER + 2 * half).astype(jnp.int32) * LANE, LANE)
    c0 = pl.multiple_of(scalar_of(msg, CORNER + 2 * half + 1).astype(jnp.int32) * LANE, LANE)
    return pl.ds(r0, WIN), pl.ds(c0, WIN)


def window_copy(msg, half, mate_ref, win, sem):
    copy = pltpu.make_async_copy(mate_ref.at[corner(msg, half)], win, sem)
    copy.start()
    return copy


def contribution(msg, half, profile, tile_ref, edge, copy=None):
    prm = msg[half * HALF : half * HALF + HALF]
    prm = jnp.concatenate([prm, profile, jnp.zeros((2, edge), f32)], axis=0)
    rmat = row_matrix(prm, edge)
    cmat = col_matrix(prm, edge)
    if copy is None:
        window = tile_ref[corner(msg, half)]
    else:
        copy.wait()
        window = tile_ref[...]
    rows = jnp.dot(rmat, window, preferred_element_type=f32).astype(bf16)
    contrib = jnp.dot(rows, cmat, preferred_element_type=f32)
    return contrib * prm.T[:, HALF : HALF + 1] * profile[1:2]


def local_pair(msg, profile, beside, tile_ref, mate_ref, win, sem, edge):
    copy = window_copy(msg, 1, mate_ref, win, sem)
    total = contribution(msg, 0, profile, tile_ref, edge)
    return total + contribution(msg, 1, beside, win, edge, copy)


def weight_sum(msg, profiles):
    edge = msg.shape[1]
    lane = lax.broadcasted_iota(jnp.int32, (1, edge), 1)
    pad = [jnp.zeros((16 - len(profiles), edge), f32)]
    rows, cols = [], []
    for n, profile in enumerate(profiles):
        used = jnp.sum(jnp.where(lane == n, msg[SCALARS : SCALARS + 1], 0.0), axis=1, keepdims=True)
        rows.append(profile[0:1])
        cols.append(profile[1:2] * used)
    rows = jnp.concatenate(rows + pad, axis=0)
    cols = jnp.concatenate(cols + pad, axis=0)
    return jnp.dot(rows.T.astype(bf16), cols.astype(bf16), preferred_element_type=f32)


def pool(block, half):
    edge = block.shape[0]
    source = lax.broadcasted_iota(jnp.int32, (edge, edge // 2), 0)
    target = lax.broadcasted_iota(jnp.int32, (edge, edge // 2), 1)
    pairs = jnp.where(lax.shift_right_logical(source, 1) == target, 0.25, 0.0).astype(bf16)
    sums = jnp.dot(block, pairs, preferred_element_type=f32)
    parts = []
    for h in range(edge // 2 // LANE):
        half[h] = sums[:, h * LANE : (h + 1) * LANE]
        parts.append(half[h, pl.ds(0, edge // 2, stride=2), :] + half[h, pl.ds(1, edge // 2, stride=2), :])
    return jnp.concatenate(parts, axis=1)


def behind(profile, edge):
    return jnp.concatenate([profile, jnp.zeros((EXTRA - 2, edge), f32)], axis=0).astype(bf16)


def own_profiles(mine_ref, theirs_ref):
    mine, theirs = mine_ref[...].astype(f32), theirs_ref[...].astype(f32)
    return mine[PROFILE : PROFILE + 2], theirs[BESIDE : BESIDE + 2]


def first_kernel(got_ref, mine_ref, theirs_ref, tile_ref, mate_ref, out_ref, win, sem):
    edge = out_ref.shape[1]
    outer = is_outer()
    profile, beside = own_profiles(mine_ref, theirs_ref)
    msg = got_ref[...].astype(f32)

    @pl.when(outer)
    def _():
        total = local_pair(msg, profile, beside, tile_ref, mate_ref, win, sem, edge)
        none = jnp.zeros_like(profile)
        theirs = [msg[PROFILE : PROFILE + 2], msg[BESIDE : BESIDE + 2], none]
        denom = weight_sum(msg, theirs + [profile, beside, none])
        out_ref[0:edge] = (total / denom).astype(bf16)
        out_ref[edge:] = jnp.zeros((EXTRA, edge), bf16)

    @pl.when(jnp.logical_not(outer))
    def _():
        out_ref[0:edge] = contribution(msg, 0, profile, tile_ref, edge).astype(bf16)
        out_ref[edge:] = behind(profile, edge)


def second_kernel(down_ref, mine_ref, theirs_ref, tile_ref, mate_ref, out_ref, win, sem):
    edge = out_ref.shape[1]
    outer = is_outer()
    profile, beside = own_profiles(mine_ref, theirs_ref)
    msg = down_ref[...].astype(f32)

    @pl.when(outer)
    def _():
        copy = window_copy(msg, 0, mate_ref, win, sem)
        out_ref[0:edge] = contribution(msg, 0, beside, win, edge, copy).astype(bf16)
        out_ref[edge:] = behind(beside, edge)

    @pl.when(jnp.logical_not(outer))
    def _():
        total = local_pair(msg, profile, beside, tile_ref, mate_ref, win, sem, edge)
        out_ref[0:edge] = total.astype(bf16)
        out_ref[edge:] = jnp.zeros((EXTRA, edge), bf16)


def merge_kernel(local_ref, over_ref, got_ref, down_ref, mine_ref, theirs_ref, out_ref, pooled_ref, half):
    edge = out_ref.shape[1]

    @pl.when(jnp.logical_not(is_outer()))
    def _():
        profile, beside = own_profiles(mine_ref, theirs_ref)
        msg = down_ref[...].astype(f32)
        across = got_ref[...].astype(f32)[PROFILE : PROFILE + 2]
        theirs = [msg[PROFILE : PROFILE + 2], msg[BESIDE : BESIDE + 2], across]
        denom = weight_sum(msg, theirs + [profile, beside, over_ref[edge:].astype(f32)[0:2]])
        total = local_ref[0:edge].astype(f32) + over_ref[0:edge].astype(f32)
        block = (total / denom).astype(bf16)
        out_ref[...] = block
        pooled_ref[...] = pool(block, half).astype(bf16)


def own_kernel(own_ref, mine_ref, theirs_ref, tile_ref, mate_ref, out_ref, win, sem):
    profile, beside = own_profiles(mine_ref, theirs_ref)
    msg = own_ref[...].astype(f32)
    out_ref[...] = local_pair(msg, profile, beside, tile_ref, mate_ref, win, sem, out_ref.shape[1])


def blend_kernel(
    local_ref, side_ref, got_ref, down_ref, mine_ref, theirs_ref, early_ref, pooled_early_ref, out_ref, pooled_ref, half
):
    edge = out_ref.shape[1]
    outer = is_outer()
    profile, beside = own_profiles(mine_ref, theirs_ref)
    got, down = got_ref[...].astype(f32), down_ref[...].astype(f32)
    msg = jnp.where(outer, got, down)
    theirs = [msg[PROFILE : PROFILE + 2], msg[BESIDE : BESIDE + 2], got[PROFILE : PROFILE + 2]]
    mine_across = side_ref[edge:].astype(f32)[0:2]
    denom = weight_sum(mine_ref[...].astype(f32), [profile, beside, mine_across] + theirs)
    total = local_ref[...] + side_ref[0:edge].astype(f32)
    early = jnp.where(outer, early_ref[0:edge].astype(f32), 0.0)
    block = total / denom + early
    out_ref[...] = block
    pooled_ref[...] = (pool(block.astype(bf16), half) + pooled_early_ref[...].astype(f32)).astype(bf16)


def last_kernel(block_ref, late_ref, out_ref):
    out_ref[...] = (block_ref[...] + late_ref[...].astype(f32)).astype(bf16)


def call(kernel, name, out_shape, operands, mate=None, halves=False, work=(1e9, 4e6)):
    single = not isinstance(out_shape, list)
    edge = (out_shape if single else out_shape[0]).shape[1]
    scratch, far = [], []
    if mate is not None:
        scratch = [pltpu.VMEM((WIN, WIN), bf16), pltpu.SemaphoreType.DMA]
        far = [pltpu.with_memory_space_constraint(mate, pltpu.HBM)]
    if halves:
        scratch = [pltpu.VMEM((edge // 2 // LANE, edge, LANE), f32)]
    return pl.pallas_call(
        kernel,
        name=name,
        out_shape=out_shape,
        in_specs=[vmem()] * len(operands) + [hbm()] * len(far),
        out_specs=vmem() if single else [vmem()] * len(out_shape),
        scratch_shapes=scratch,
        compiler_params=pltpu.CompilerParams(vmem_limit_bytes=WORK_VMEM),
        cost_estimate=cost(*work),
    )(*[pltpu.with_memory_space_constraint(x, pltpu.VMEM) for x in operands], *far)


def two_row_device(
    tiles, row_taps, col_taps, row_starts, col_starts, feather_rows, feather_cols, footprint, offsets
):
    tile = tiles[0, 0]
    edge = row_starts.shape[3]
    devices = lax.axis_size("blk")

    def send(value, pairs):
        return lax.ppermute(value, "blk", pairs)

    def swap(pairs):
        return [(i, j) for i, j in pairs] + [(j, i) for i, j in pairs]

    in_chip = [(i, i ^ 1) for i in range(devices)]
    vertical_outer = swap([(0, 4), (3, 7)])
    vertical_inner = swap([(1, 5), (2, 6)])
    diagonal = swap([(1, 6), (2, 5)])
    across_inner = swap([(1, 2), (5, 6)])
    across_outer = swap([(0, 3), (4, 7)])
    outer_to_inner = [(0, 2), (3, 1), (4, 6), (7, 5)]

    mine, diag, aside, own_msg = prepare(
        row_taps[0, 0],
        col_taps[0, 0],
        row_starts.reshape(-1, 1, edge),
        col_starts.reshape(-1, 1, edge),
        footprint[0],
        offsets[0, 0].T,
        feather_rows[0],
        feather_cols[0],
    )
    theirs = send(aside, in_chip)
    theirs, tile_after = lax.optimization_barrier((theirs, tile))
    mate = send(tile_after, in_chip)
    near = fetch(tile)
    outer = is_outer()
    row = lax.broadcasted_iota(jnp.int32, mine.shape, 0)
    from_beside = jnp.logical_and(row >= BESIDE, row < BESIDE + 2)
    asking = jnp.where(from_beside, theirs, mine)
    got = send(jnp.where(outer, asking, diag), vertical_outer + diagonal)
    down = send(jnp.where(outer, theirs, asking), across_outer + vertical_inner)

    block = jax.ShapeDtypeStruct((edge + EXTRA, edge), bf16)
    bare = jax.ShapeDtypeStruct((edge, edge), bf16)
    bare32 = jax.ShapeDtypeStruct((edge, edge), f32)
    pooled = jax.ShapeDtypeStruct((edge // 2, edge // 2), bf16)
    two = (4e9, 4e6)

    got, down = lax.optimization_barrier((got, down))
    first = call(first_kernel, "first", block, (got, mine, theirs, near), mate, work=two)
    early = send(first, vertical_outer + across_inner)
    second = call(second_kernel, "second", block, (down, mine, theirs, near), mate, work=two)
    second, early = lax.optimization_barrier((second, early))
    side = send(second, outer_to_inner)
    late_out, pooled_out = call(
        merge_kernel, "merge", [bare, pooled], (second, early, got, down, mine, theirs), halves=True
    )
    pooled_late = send(pooled_out, vertical_inner)
    late = send(late_out, vertical_inner)
    local = call(own_kernel, "own", bare32, (own_msg, mine, theirs, near), mate, work=two)
    block_so_far, pooled_all = call(
        blend_kernel,
        "blend",
        [bare32, pooled],
        (local, side, got, down, mine, theirs, early, pooled_late),
        halves=True,
    )
    sections = lax.axis_size("sec")
    before = lax.ppermute(pooled_all, "sec", [(i, i + 1) for i in range(sections - 1)])
    after = lax.ppermute(pooled_all, "sec", [(i + 1, i) for i in range(sections - 1)])
    blended = call(last_kernel, "last", bare, (block_so_far, late), work=(1e6, 2e6))
    index = lax.axis_index("sec")
    present = 4.0 - (index == 0).astype(f32) - (index == sections - 1).astype(f32)
    level = (before.astype(f32) + 2.0 * pooled_all.astype(f32) + after.astype(f32)) / present
    return blended[None, None], level.astype(bf16)[None, None]


def per_device(*args):
    if lax.axis_size("blk") == 2 * GY:
        return two_row_device(*args)
    return general_device(*args)


def solution(mesh):
    return jax.shard_map(
        per_device,
        mesh=mesh,
        in_specs=(
            P("sec", "blk", None, None),
            P("sec", "blk", None, None, None),
            P("sec", "blk", None, None, None),
            P("sec", "blk", None, None),
            P("sec", "blk", None, None),
            P("sec", "blk", None),
            P("sec", "blk", None),
            P("sec", "blk", None),
            P("sec", "blk", None, None),
        ),
        out_specs=(P("sec", "blk", None, None), P("sec", "blk", None, None)),
        check_vma=False,
    )
```

```python
import functools

import jax
import jax.numpy as jnp
from jax import lax
from jax.experimental import pallas as pl
from jax.experimental.pallas import tpu as pltpu
from jax.sharding import PartitionSpec as P

BAND = 640
GY = 4
TAPS = 4
LANE = 128
WIN = BAND + LANE
EXTRA = 16
VMEM_LIMIT = 40 * 1024 * 1024

bf16 = jnp.bfloat16
f32 = jnp.float32


def vmem():
    return pl.BlockSpec(memory_space=pltpu.VMEM)


def smem():
    return pl.BlockSpec(memory_space=pltpu.SMEM)


def hbm():
    return pl.BlockSpec(memory_space=pltpu.HBM)


def params():
    return pltpu.CompilerParams(vmem_limit_bytes=VMEM_LIMIT)


def cost(flops, nbytes):
    return pl.CostEstimate(flops=int(flops), bytes_accessed=int(nbytes), transcendentals=0)


def slot_of(column, role, step):
    odd = column % 2
    if role == 0:
        across = 0
    elif role == 1:
        across = 1 - 2 * odd
    else:
        across = 2 * odd - 1
    return 3 * (across + 1) + (step + 1)


def my_column():
    return lax.rem(lax.axis_index("blk"), GY)


def my_row():
    return lax.div(lax.axis_index("blk"), GY)


def step_of(move):
    if move == "swap":
        return 1 - 2 * my_row()
    return -move


def pack_kernel(moves, rt_ref, ct_ref, rs_ref, cs_ref, foot_ref, off_ref, fr_ref, fc_ref, tile_ref, *refs):
    outs, (buf, fbuf, sems) = refs[:-3], refs[-3:]
    ext_ref, packed = outs[0], outs[1:]
    size = tile_ref.shape[0]
    whole = pltpu.make_async_copy(tile_ref, ext_ref.at[pl.ds(0, size)], sems.at[0])
    whole.start()
    edge = fr_ref.shape[1]
    fbuf[...] = jnp.zeros(fbuf.shape, bf16)
    fbuf[0:1, 0:edge] = fr_ref[...]
    fbuf[0:1, edge : 2 * edge] = fc_ref[...]
    tail = pltpu.make_async_copy(fbuf, ext_ref.at[pl.ds(size, EXTRA)], sems.at[1])
    tail.start()
    column = my_column()
    most = (size - BAND) // LANE - 1
    steps = [0] + [step_of(move) for move in moves]
    for group, step in enumerate(steps):
        for role in range(3):
            k = jnp.clip(slot_of(column, role, step), 0, 8)
            used = foot_ref[k].astype(f32)
            buf[0:TAPS] = rt_ref[k].astype(f32)
            buf[TAPS : 2 * TAPS] = ct_ref[k].astype(f32) * used
            for dim, ref in enumerate((rs_ref, cs_ref)):
                off = off_ref[2 * k + dim]
                base = jnp.minimum(lax.div(off, LANE), most)
                rel = ref[pl.ds(k, 1), :] + (off - base * LANE)
                high = lax.shift_right_logical(rel, 5)
                buf[8 + 2 * dim : 9 + 2 * dim] = high.astype(f32)
                buf[9 + 2 * dim : 10 + 2 * dim] = (rel - high * 32).astype(f32)
                buf[12 + dim : 13 + dim] = jnp.zeros((1, edge), f32) + base.astype(f32)
            buf[14:16] = jnp.zeros((2, edge), f32)
            packed[group][role] = buf[...].astype(bf16)
    whole.wait()
    tail.wait()


def pack(moves, rt, ct, rs, cs, foot, off, fr, fc, tile):
    size, edge = tile.shape[0], rs.shape[1]
    groups = 1 + len(moves)
    return pl.pallas_call(
        functools.partial(pack_kernel, moves),
        name="pack",
        out_shape=[jax.ShapeDtypeStruct((size + EXTRA, tile.shape[1]), bf16)]
        + [jax.ShapeDtypeStruct((3, 16, edge), bf16)] * groups,
        in_specs=[vmem()] * 4 + [smem()] * 2 + [vmem()] * 2 + [hbm()],
        out_specs=[hbm()] + [vmem()] * groups,
        scratch_shapes=[
            pltpu.VMEM((16, edge), f32),
            pltpu.VMEM((EXTRA, tile.shape[1]), bf16),
            pltpu.SemaphoreType.DMA((2,)),
        ],
        compiler_params=params(),
        cost_estimate=cost(1e6, 5e6),
    )(rt, ct, rs, cs, foot, off, fr, fc, tile)


def row_matrix(prm, edge):
    cols = prm.T
    rel = cols[:, 8:9] * 32.0 + cols[:, 9:10]
    rel = jnp.broadcast_to(rel, (edge, LANE))
    taps = [jnp.broadcast_to(cols[:, q : q + 1], (edge, LANE)).astype(bf16) for q in range(TAPS)]
    lane = lax.broadcasted_iota(jnp.int32, (edge, LANE), 1).astype(f32)
    parts = []
    for h in range(WIN // LANE):
        place = ((lane + float(LANE * h)) - rel).astype(bf16)
        part = jnp.zeros((edge, LANE), bf16)
        for q in range(TAPS):
            part = jnp.where(place == bf16(q), taps[q], part)
        parts.append(part)
    return jnp.concatenate(parts, axis=1)


def col_matrix(prm, edge):
    rel = prm[10:11] * 32.0 + prm[11:12]
    taps = [jnp.broadcast_to(prm[TAPS + q : TAPS + q + 1], (LANE, edge)).astype(bf16) for q in range(TAPS)]
    sub = lax.broadcasted_iota(jnp.int32, (LANE, edge), 0).astype(f32)
    parts = []
    for h in range(WIN // LANE):
        place = (sub - (rel - float(LANE * h))).astype(bf16)
        part = jnp.zeros((LANE, edge), bf16)
        for q in range(TAPS):
            part = jnp.where(place == bf16(q), taps[q], part)
        parts.append(part)
    return jnp.concatenate(parts, axis=0)


def contrib_kernel(slots, only_middle, feather_row, prm_ref, *refs):
    count = len(slots)
    tiles, out_ref = refs[:count], refs[count]
    win, fth, sems = refs[count + 1 :]
    edge = out_ref.shape[1]
    size = tiles[0].shape[0] - EXTRA

    def work():
        copies = []
        for s, slot in enumerate(slots):
            base = prm_ref[slot].astype(f32)
            r0 = pl.multiple_of(jnp.max(base[12:13, 0:LANE]).astype(jnp.int32) * LANE, LANE)
            c0 = pl.multiple_of(jnp.max(base[13:14, 0:LANE]).astype(jnp.int32) * LANE, LANE)
            window = pltpu.make_async_copy(
                tiles[s].at[pl.ds(r0, WIN), pl.ds(c0, WIN)], win.at[s], sems.at[s, 0]
            )
            feather = pltpu.make_async_copy(tiles[s].at[pl.ds(size, EXTRA)], fth.at[s], sems.at[s, 1])
            window.start()
            feather.start()
            copies.append((window, feather))
        total = None
        profiles = []
        for s, slot in enumerate(slots):
            prm = prm_ref[slot].astype(f32)
            rmat = row_matrix(prm, edge)
            cmat = col_matrix(prm, edge)
            copies[s][0].wait()
            copies[s][1].wait()
            rows = jnp.dot(rmat, win[s], preferred_element_type=f32).astype(bf16)
            contrib = jnp.dot(rows, cmat, preferred_element_type=f32)
            profile = fth[s].astype(f32)
            profiles += [profile[0:1, :edge], profile[0:1, edge:]]
            contrib = contrib * profile[:, :edge].T[:, 0:1] * profile[0:1, edge:]
            total = contrib if total is None else total + contrib
        out_ref[0:edge] = total.astype(out_ref.dtype)
        before = [jnp.zeros((feather_row, edge), f32)] if feather_row else []
        after = [jnp.zeros((EXTRA - feather_row - len(profiles), edge), f32)]
        out_ref[edge:] = jnp.concatenate(before + profiles + after, axis=0).astype(out_ref.dtype)

    if only_middle:
        column = my_column()
        pl.when(jnp.logical_and(column > 0, column < GY - 1))(work)
    else:
        work()


def contributions(name, prm, slots, tiles, edge, only_middle=False, feather_row=0):
    count = len(slots)
    return pl.pallas_call(
        functools.partial(contrib_kernel, slots, only_middle, feather_row),
        name=name,
        out_shape=jax.ShapeDtypeStruct((edge + EXTRA, edge), bf16),
        in_specs=[vmem()] + [hbm()] * count,
        out_specs=vmem(),
        scratch_shapes=[
            pltpu.VMEM((count, WIN, WIN), bf16),
            pltpu.VMEM((count, EXTRA, tiles[0].shape[1]), bf16),
            pltpu.SemaphoreType.DMA((count, 2)),
        ],
        compiler_params=params(),
        cost_estimate=cost(1.0e9 * count * 2, 1.2e6 * count + 5e5),
    )(prm, *tiles)


def weights_of(foot_ref, column, step, rows, roles):
    total = None
    cols = rows.T
    for role in roles:
        slot = slot_of(column, role, step)
        inside = jnp.logical_and(slot >= 0, slot < 9)
        used = jnp.where(inside, foot_ref[jnp.clip(slot, 0, 8)], 0).astype(f32)
        term = cols[:, 2 * role : 2 * role + 1] * (rows[2 * role + 1 : 2 * role + 2] * used)
        total = term if total is None else total + term
    return total


def same_row_kernel(foot_ref, own_ref, cross_ref, numer_ref, denom_ref):
    edge = own_ref.shape[1]
    rows = own_ref[edge:].astype(f32) + cross_ref[edge:].astype(f32)
    numer_ref[...] = own_ref[0:edge].astype(f32) + cross_ref[0:edge].astype(f32)
    denom_ref[...] = weights_of(foot_ref, my_column(), 0, rows, range(3))


def same_row(foot, own, cross, edge):
    return pl.pallas_call(
        same_row_kernel,
        name="same_row",
        out_shape=[jax.ShapeDtypeStruct((edge, edge), f32)] * 2,
        in_specs=[smem(), vmem(), vmem()],
        out_specs=[vmem(), vmem()],
        compiler_params=params(),
        cost_estimate=cost(4e6, 3e6),
    )(foot, own, cross)


def finish_kernel(moves, foot_ref, numer_ref, denom_ref, *refs):
    arrived, (blended_ref, pooled_ref, half) = refs[:-3], refs[-3:]
    edge = numer_ref.shape[0]
    numer, denom = numer_ref[...], denom_ref[...]
    for n, move in enumerate(moves):
        first, second = arrived[2 * n], arrived[2 * n + 1]
        numer = numer + (first[0:edge].astype(f32) + second[0:edge].astype(f32))
        rows = first[edge:].astype(f32) + second[edge:].astype(f32)
        denom = denom + weights_of(foot_ref, my_column(), step_of(move), rows, range(3))
    blended = (numer / denom).astype(bf16)
    blended_ref[...] = blended
    source = lax.broadcasted_iota(jnp.int32, (edge, edge // 2), 0)
    target = lax.broadcasted_iota(jnp.int32, (edge, edge // 2), 1)
    pairs = jnp.where(lax.shift_right_logical(source, 1) == target, 1.0, 0.0).astype(bf16)
    pooled = jnp.dot(blended, pairs, preferred_element_type=f32) * 0.25
    for h in range(edge // 2 // LANE):
        half[h] = pooled[:, h * LANE : (h + 1) * LANE]
        total = half[h, pl.ds(0, edge // 2, stride=2), :] + half[h, pl.ds(1, edge // 2, stride=2), :]
        pooled_ref[:, h * LANE : (h + 1) * LANE] = total.astype(bf16)


def finish(moves, foot, numer, denom, arrived, edge):
    return pl.pallas_call(
        functools.partial(finish_kernel, moves),
        name="finish",
        out_shape=[
            jax.ShapeDtypeStruct((edge, edge), bf16),
            jax.ShapeDtypeStruct((edge // 2, edge // 2), bf16),
        ],
        in_specs=[smem(), vmem(), vmem()] + [vmem()] * len(arrived),
        out_specs=[vmem(), vmem()],
        scratch_shapes=[pltpu.VMEM((edge // 2 // LANE, edge, LANE), f32)],
        compiler_params=params(),
        cost_estimate=cost(3e8, 4e6),
    )(foot, numer, denom, *arrived)


def general_device(
    tiles, row_taps, col_taps, row_starts, col_starts, feather_rows, feather_cols, footprint, offsets
):
    tile = tiles[0, 0]
    edge = row_starts.shape[3]
    devices = lax.axis_size("blk")
    rows = devices // GY
    moves = ["swap"] if rows == 2 else [1, -1]
    foot = footprint.reshape(9)

    def along(move, value, columns=range(GY), back=False):
        pairs = []
        for r in range(rows):
            to = (1 - r) if move == "swap" else r + (-move if back else move)
            if 0 <= to < rows:
                pairs += [(r * GY + c, to * GY + c) for c in columns]
        return lax.ppermute(value, "blk", pairs)

    def mate(value):
        return lax.ppermute(value, "blk", [(i, i ^ 1) for i in range(devices)])

    def cross(value):
        pairs = []
        for r in range(rows):
            for c in range(1, GY - 1, 2):
                pairs += [(r * GY + c, r * GY + c + 1), (r * GY + c + 1, r * GY + c)]
        return lax.ppermute(value, "blk", pairs)

    packed = pack(
        moves,
        row_taps[0, 0],
        col_taps[0, 0],
        row_starts[0, 0],
        col_starts[0, 0],
        foot,
        offsets.reshape(18),
        feather_rows[0],
        feather_cols[0],
        tile,
    )
    ext, own_prm, move_prm = packed[0], packed[1], packed[2:]
    ext_mate = mate(ext)
    asked = [along(move, prm, back=True) for move, prm in zip(moves, move_prm)]
    cross_prm = cross(jnp.stack([own_prm[2]] + [prm[2] for prm in asked]))
    arrived = []
    for n, move in enumerate(moves):
        over = contributions("cross_sum", cross_prm, [1 + n], [ext], edge, True, 4)
        over = cross(over)
        local = contributions("local_sum", asked[n], [0, 1], [ext, ext_mate], edge)
        arrived.append(along(move, local, [0, GY - 1]))
        arrived.append(along(move, local + over, range(1, GY - 1)))
    side = cross(contributions("cross_own", cross_prm, [0], [ext], edge, True, 4))
    own = contributions("local_own", own_prm, [0, 1], [ext, ext_mate], edge)
    numer, denom = same_row(foot, own, side, edge)
    blended, pooled = finish(moves, foot, numer, denom, arrived, edge)
    sections = lax.axis_size("sec")
    before = lax.ppermute(pooled, "sec", [(i, i + 1) for i in range(sections - 1)])
    after = lax.ppermute(pooled, "sec", [(i + 1, i) for i in range(sections - 1)])
    index = lax.axis_index("sec")
    present = 4.0 - (index == 0).astype(f32) - (index == sections - 1).astype(f32)
    level = (before.astype(f32) + 2.0 * pooled.astype(f32) + after.astype(f32)) / present
    return blended[None, None], level.astype(bf16)[None, None]


HALF = 12
PROFILE = 24
BESIDE = 26
SCALARS = 28
CORNER = 8
ROWS = 32
TILE = 1024
PREPARE_VMEM = 40 * 1024 * 1024
WORK_VMEM = 40 * 1024 * 1024


def is_outer():
    column = my_column()
    return jnp.logical_or(column == 0, column == GY - 1)


def prepare_kernel(rt_hbm, ct_hbm, rs_hbm, cs_hbm, foot_hbm, off_hbm, fr_hbm, fc_hbm, *refs):
    outs = refs[:4]
    rt_ref, ct_ref, rs_ref, cs_ref, fr_ref, fc_ref, foot_ref, off_ref, buf, sems = refs[4:]
    pairs = [
        (off_hbm, off_ref),
        (foot_hbm, foot_ref),
        (rt_hbm, rt_ref),
        (ct_hbm, ct_ref),
        (rs_hbm, rs_ref),
        (cs_hbm, cs_ref),
        (fr_hbm, fr_ref),
        (fc_hbm, fc_ref),
    ]
    copies = [pltpu.make_async_copy(a, b, sems.at[i]) for i, (a, b) in enumerate(pairs)]
    for copy in copies:
        copy.start()
    for copy in copies:
        copy.wait()
    edge = fr_ref.shape[1]
    column = my_column()
    over = 1 - 2 * my_row()
    most = (TILE - BAND) // LANE - 1
    lane = lax.broadcasted_iota(jnp.int32, (1, edge), 1)
    scalars = jnp.zeros((1, edge), f32)
    for n in range(6):
        slot = slot_of(column, n % 3, 0 if n < 3 else over)
        inside = jnp.logical_and(slot >= 0, slot < 9)
        used = jnp.where(inside, foot_ref[0, jnp.clip(slot, 0, 8)], 0).astype(f32)
        scalars = jnp.where(lane == n, used, scalars)

    def message(out_ref, slots, profile_row):
        row = scalars
        buf[...] = jnp.zeros(buf.shape, f32)
        for half, (role, step) in enumerate(slots):
            k = jnp.clip(slot_of(column, role, step), 0, 8)
            used = foot_ref[0, k].astype(f32)
            at = half * HALF
            buf[at : at + TAPS] = rt_ref[k].astype(f32)
            buf[at + TAPS : at + 2 * TAPS] = ct_ref[k].astype(f32) * used
            for dim, ref in enumerate((rs_ref, cs_ref)):
                off = off_ref[dim, k]
                base = jnp.minimum(lax.div(off, LANE), most)
                rel = ref[k] + (off - base * LANE)
                high = lax.shift_right_logical(rel, 5)
                first = at + 2 * TAPS + 2 * dim
                buf[first : first + 1] = high.astype(f32)
                buf[first + 1 : first + 2] = (rel - high * 32).astype(f32)
                row = jnp.where(lane == CORNER + 2 * half + dim, base.astype(f32), row)
        buf[profile_row : profile_row + 1] = fr_ref[...].astype(f32)
        buf[profile_row + 1 : profile_row + 2] = fc_ref[...].astype(f32)
        buf[SCALARS : SCALARS + 1] = row
        out_ref[...] = buf[...].astype(bf16)

    message(outs[0], [(0, over), (1, over)], PROFILE)
    message(outs[1], [(2, over)], PROFILE)
    message(outs[2], [(2, 0)], BESIDE)
    message(outs[3], [(0, 0), (1, 0)], PROFILE)


def prepare(rt, ct, rs, cs, foot, off, fr, fc):
    edge = fr.shape[1]
    args = [pltpu.with_memory_space_constraint(x, pltpu.HBM) for x in (rt, ct, rs, cs, foot, off, fr, fc)]
    return pl.pallas_call(
        prepare_kernel,
        name="prepare",
        out_shape=[jax.ShapeDtypeStruct((ROWS, edge), bf16)] * 4,
        in_specs=[hbm()] * 8,
        out_specs=[vmem()] * 4,
        scratch_shapes=[pltpu.VMEM(x.shape, x.dtype) for x in (rt, ct, rs, cs, fr, fc)]
        + [pltpu.SMEM(x.shape, x.dtype) for x in (foot, off)]
        + [pltpu.VMEM((ROWS, edge), f32), pltpu.SemaphoreType.DMA((8,))],
        compiler_params=pltpu.CompilerParams(vmem_limit_bytes=PREPARE_VMEM),
        cost_estimate=cost(1e6, 2e5),
    )(*args)


def fetch_kernel(tile_ref, out_ref, sems):
    parts = sems.shape[0]
    size = out_ref.shape[0] // parts
    copies = [
        pltpu.make_async_copy(tile_ref.at[pl.ds(n * size, size)], out_ref.at[pl.ds(n * size, size)], sems.at[n])
        for n in range(parts)
    ]
    for copy in copies:
        copy.start()
    for copy in copies:
        copy.wait()


def fetch(tile):
    return pl.pallas_call(
        fetch_kernel,
        name="fetch",
        out_shape=pltpu.VMEM(tile.shape, tile.dtype),
        in_specs=[hbm()],
        out_specs=vmem(),
        scratch_shapes=[pltpu.SemaphoreType.DMA((8,))],
        compiler_params=pltpu.CompilerParams(vmem_limit_bytes=PREPARE_VMEM),
        cost_estimate=cost(1e6, 4e6),
    )(pltpu.with_memory_space_constraint(tile, pltpu.HBM))


def scalar_of(msg, n):
    lane = lax.broadcasted_iota(jnp.int32, (1, LANE), 1)
    return jnp.sum(jnp.where(lane == n, msg[SCALARS : SCALARS + 1, 0:LANE], 0.0))


def corner(msg, half):
    r0 = pl.multiple_of(scalar_of(msg, CORNER + 2 * half).astype(jnp.int32) * LANE, LANE)
    c0 = pl.multiple_of(scalar_of(msg, CORNER + 2 * half + 1).astype(jnp.int32) * LANE, LANE)
    return pl.ds(r0, WIN), pl.ds(c0, WIN)


def window_copy(msg, half, mate_ref, win, sem):
    copy = pltpu.make_async_copy(mate_ref.at[corner(msg, half)], win, sem)
    copy.start()
    return copy


def contribution(msg, half, profile, tile_ref, edge, copy=None):
    prm = msg[half * HALF : half * HALF + HALF]
    prm = jnp.concatenate([prm, profile, jnp.zeros((2, edge), f32)], axis=0)
    rmat = row_matrix(prm, edge)
    cmat = col_matrix(prm, edge)
    if copy is None:
        window = tile_ref[corner(msg, half)]
    else:
        copy.wait()
        window = tile_ref[...]
    rows = jnp.dot(rmat, window, preferred_element_type=f32).astype(bf16)
    contrib = jnp.dot(rows, cmat, preferred_element_type=f32)
    return contrib * prm.T[:, HALF : HALF + 1] * profile[1:2]


def local_pair(msg, profile, beside, tile_ref, mate_ref, win, sem, edge):
    copy = window_copy(msg, 1, mate_ref, win, sem)
    total = contribution(msg, 0, profile, tile_ref, edge)
    return total + contribution(msg, 1, beside, win, edge, copy)


def weight_sum(msg, profiles):
    edge = msg.shape[1]
    lane = lax.broadcasted_iota(jnp.int32, (1, edge), 1)
    pad = [jnp.zeros((16 - len(profiles), edge), f32)]
    rows, cols = [], []
    for n, profile in enumerate(profiles):
        used = jnp.sum(jnp.where(lane == n, msg[SCALARS : SCALARS + 1], 0.0), axis=1, keepdims=True)
        rows.append(profile[0:1])
        cols.append(profile[1:2] * used)
    rows = jnp.concatenate(rows + pad, axis=0)
    cols = jnp.concatenate(cols + pad, axis=0)
    return jnp.dot(rows.T.astype(bf16), cols.astype(bf16), preferred_element_type=f32)


def pool(block, half):
    edge = block.shape[0]
    source = lax.broadcasted_iota(jnp.int32, (edge, edge // 2), 0)
    target = lax.broadcasted_iota(jnp.int32, (edge, edge // 2), 1)
    pairs = jnp.where(lax.shift_right_logical(source, 1) == target, 0.25, 0.0).astype(bf16)
    sums = jnp.dot(block, pairs, preferred_element_type=f32)
    parts = []
    for h in range(edge // 2 // LANE):
        half[h] = sums[:, h * LANE : (h + 1) * LANE]
        parts.append(half[h, pl.ds(0, edge // 2, stride=2), :] + half[h, pl.ds(1, edge // 2, stride=2), :])
    return jnp.concatenate(parts, axis=1)


def behind(profile, edge):
    return jnp.concatenate([profile, jnp.zeros((EXTRA - 2, edge), f32)], axis=0).astype(bf16)


def own_profiles(mine_ref, theirs_ref):
    mine, theirs = mine_ref[...].astype(f32), theirs_ref[...].astype(f32)
    return mine[PROFILE : PROFILE + 2], theirs[BESIDE : BESIDE + 2]


def first_kernel(got_ref, mine_ref, theirs_ref, tile_ref, mate_ref, out_ref, win, sem):
    edge = out_ref.shape[1]
    outer = is_outer()
    profile, beside = own_profiles(mine_ref, theirs_ref)
    msg = got_ref[...].astype(f32)

    @pl.when(outer)
    def _():
        total = local_pair(msg, profile, beside, tile_ref, mate_ref, win, sem, edge)
        none = jnp.zeros_like(profile)
        theirs = [msg[PROFILE : PROFILE + 2], msg[BESIDE : BESIDE + 2], none]
        denom = weight_sum(msg, theirs + [profile, beside, none])
        out_ref[0:edge] = (total / denom).astype(bf16)
        out_ref[edge:] = jnp.zeros((EXTRA, edge), bf16)

    @pl.when(jnp.logical_not(outer))
    def _():
        out_ref[0:edge] = contribution(msg, 0, profile, tile_ref, edge).astype(bf16)
        out_ref[edge:] = behind(profile, edge)


def second_kernel(down_ref, mine_ref, theirs_ref, tile_ref, mate_ref, out_ref, win, sem):
    edge = out_ref.shape[1]
    outer = is_outer()
    profile, beside = own_profiles(mine_ref, theirs_ref)
    msg = down_ref[...].astype(f32)

    @pl.when(outer)
    def _():
        copy = window_copy(msg, 0, mate_ref, win, sem)
        out_ref[0:edge] = contribution(msg, 0, beside, win, edge, copy).astype(bf16)
        out_ref[edge:] = behind(beside, edge)

    @pl.when(jnp.logical_not(outer))
    def _():
        total = local_pair(msg, profile, beside, tile_ref, mate_ref, win, sem, edge)
        out_ref[0:edge] = total.astype(bf16)
        out_ref[edge:] = jnp.zeros((EXTRA, edge), bf16)


def merge_kernel(local_ref, over_ref, got_ref, down_ref, mine_ref, theirs_ref, out_ref, pooled_ref, half):
    edge = out_ref.shape[1]

    @pl.when(jnp.logical_not(is_outer()))
    def _():
        profile, beside = own_profiles(mine_ref, theirs_ref)
        msg = down_ref[...].astype(f32)
        across = got_ref[...].astype(f32)[PROFILE : PROFILE + 2]
        theirs = [msg[PROFILE : PROFILE + 2], msg[BESIDE : BESIDE + 2], across]
        denom = weight_sum(msg, theirs + [profile, beside, over_ref[edge:].astype(f32)[0:2]])
        total = local_ref[0:edge].astype(f32) + over_ref[0:edge].astype(f32)
        block = (total / denom).astype(bf16)
        out_ref[...] = block
        pooled_ref[...] = pool(block, half).astype(bf16)


def own_kernel(own_ref, mine_ref, theirs_ref, tile_ref, mate_ref, out_ref, win, sem):
    profile, beside = own_profiles(mine_ref, theirs_ref)
    msg = own_ref[...].astype(f32)
    out_ref[...] = local_pair(msg, profile, beside, tile_ref, mate_ref, win, sem, out_ref.shape[1])


def blend_kernel(
    local_ref, side_ref, got_ref, down_ref, mine_ref, theirs_ref, early_ref, pooled_early_ref, out_ref, pooled_ref, half
):
    edge = out_ref.shape[1]
    outer = is_outer()
    profile, beside = own_profiles(mine_ref, theirs_ref)
    got, down = got_ref[...].astype(f32), down_ref[...].astype(f32)
    msg = jnp.where(outer, got, down)
    theirs = [msg[PROFILE : PROFILE + 2], msg[BESIDE : BESIDE + 2], got[PROFILE : PROFILE + 2]]
    mine_across = side_ref[edge:].astype(f32)[0:2]
    denom = weight_sum(mine_ref[...].astype(f32), [profile, beside, mine_across] + theirs)
    total = local_ref[...] + side_ref[0:edge].astype(f32)
    early = jnp.where(outer, early_ref[0:edge].astype(f32), 0.0)
    block = total / denom + early
    out_ref[...] = block
    pooled_ref[...] = (pool(block.astype(bf16), half) + pooled_early_ref[...].astype(f32)).astype(bf16)


def last_kernel(block_ref, late_ref, out_ref):
    out_ref[...] = (block_ref[...] + late_ref[...].astype(f32)).astype(bf16)


def call(kernel, name, out_shape, operands, mate=None, halves=False, work=(1e9, 4e6)):
    single = not isinstance(out_shape, list)
    edge = (out_shape if single else out_shape[0]).shape[1]
    scratch, far = [], []
    if mate is not None:
        scratch = [pltpu.VMEM((WIN, WIN), bf16), pltpu.SemaphoreType.DMA]
        far = [pltpu.with_memory_space_constraint(mate, pltpu.HBM)]
    if halves:
        scratch = [pltpu.VMEM((edge // 2 // LANE, edge, LANE), f32)]
    return pl.pallas_call(
        kernel,
        name=name,
        out_shape=out_shape,
        in_specs=[vmem()] * len(operands) + [hbm()] * len(far),
        out_specs=vmem() if single else [vmem()] * len(out_shape),
        scratch_shapes=scratch,
        compiler_params=pltpu.CompilerParams(vmem_limit_bytes=WORK_VMEM),
        cost_estimate=cost(*work),
    )(*[pltpu.with_memory_space_constraint(x, pltpu.VMEM) for x in operands], *far)


def two_row_device(
    tiles, row_taps, col_taps, row_starts, col_starts, feather_rows, feather_cols, footprint, offsets
):
    tile = tiles[0, 0]
    edge = row_starts.shape[3]
    devices = lax.axis_size("blk")

    def send(value, pairs):
        return lax.ppermute(value, "blk", pairs)

    def swap(pairs):
        return [(i, j) for i, j in pairs] + [(j, i) for i, j in pairs]

    in_chip = [(i, i ^ 1) for i in range(devices)]
    vertical_outer = swap([(0, 4), (3, 7)])
    vertical_inner = swap([(1, 5), (2, 6)])
    diagonal = swap([(1, 6), (2, 5)])
    across_inner = swap([(1, 2), (5, 6)])
    across_outer = swap([(0, 3), (4, 7)])
    outer_to_inner = [(0, 2), (3, 1), (4, 6), (7, 5)]

    mine, diag, aside, own_msg = prepare(
        row_taps[0, 0],
        col_taps[0, 0],
        row_starts.reshape(-1, 1, edge),
        col_starts.reshape(-1, 1, edge),
        footprint[0],
        offsets[0, 0].T,
        feather_rows[0],
        feather_cols[0],
    )
    theirs = send(aside, in_chip)
    theirs, tile_after = lax.optimization_barrier((theirs, tile))
    mate = send(tile_after, in_chip)
    near = fetch(tile)
    outer = is_outer()
    row = lax.broadcasted_iota(jnp.int32, mine.shape, 0)
    from_beside = jnp.logical_and(row >= BESIDE, row < BESIDE + 2)
    asking = jnp.where(from_beside, theirs, mine)
    got = send(jnp.where(outer, asking, diag), vertical_outer + diagonal)
    down = send(jnp.where(outer, theirs, asking), across_outer + vertical_inner)

    block = jax.ShapeDtypeStruct((edge + EXTRA, edge), bf16)
    bare = jax.ShapeDtypeStruct((edge, edge), bf16)
    bare32 = jax.ShapeDtypeStruct((edge, edge), f32)
    pooled = jax.ShapeDtypeStruct((edge // 2, edge // 2), bf16)
    two = (4e9, 4e6)
    tiny = (1e4, 1e4)

    first = call(first_kernel, "first", block, (got, mine, theirs, near), mate, work=tiny)
    early = send(first, vertical_outer + across_inner)
    down, first = lax.optimization_barrier((down, first))
    second = call(second_kernel, "second", block, (down, mine, theirs, near), mate, work=two)
    own_msg, second = lax.optimization_barrier((own_msg, second))
    local = call(own_kernel, "own", bare32, (own_msg, mine, theirs, near), mate, work=two)
    second, local = lax.optimization_barrier((second, local))
    side = send(second, outer_to_inner)
    early, local = lax.optimization_barrier((early, local))
    late_out, pooled_out = call(
        merge_kernel, "merge", [bare, pooled], (second, early, got, down, mine, theirs), halves=True
    )
    pooled_late = send(pooled_out, vertical_inner)
    late = send(late_out, vertical_inner)
    block_so_far, pooled_all = call(
        blend_kernel,
        "blend",
        [bare32, pooled],
        (local, side, got, down, mine, theirs, early, pooled_late),
        halves=True,
    )
    sections = lax.axis_size("sec")
    before = lax.ppermute(pooled_all, "sec", [(i, i + 1) for i in range(sections - 1)])
    after = lax.ppermute(pooled_all, "sec", [(i + 1, i) for i in range(sections - 1)])
    blended = call(last_kernel, "last", bare, (block_so_far, late), work=(1e6, 2e6))
    index = lax.axis_index("sec")
    present = 4.0 - (index == 0).astype(f32) - (index == sections - 1).astype(f32)
    level = (before.astype(f32) + 2.0 * pooled_all.astype(f32) + after.astype(f32)) / present
    return blended[None, None], level.astype(bf16)[None, None]


def per_device(*args):
    if lax.axis_size("blk") == 2 * GY:
        return two_row_device(*args)
    return general_device(*args)


def solution(mesh):
    return jax.shard_map(
        per_device,
        mesh=mesh,
        in_specs=(
            P("sec", "blk", None, None),
            P("sec", "blk", None, None, None),
            P("sec", "blk", None, None, None),
            P("sec", "blk", None, None),
            P("sec", "blk", None, None),
            P("sec", "blk", None),
            P("sec", "blk", None),
            P("sec", "blk", None),
            P("sec", "blk", None, None),
        ),
        out_specs=(P("sec", "blk", None, None), P("sec", "blk", None, None)),
        check_vma=False,
    )
```

```python
import functools

import jax
import jax.numpy as jnp
from jax import lax
from jax.experimental import pallas as pl
from jax.experimental.pallas import tpu as pltpu
from jax.sharding import PartitionSpec as P

BAND = 640
GY = 4
TAPS = 4
LANE = 128
WIN = BAND + LANE
EXTRA = 16
VMEM_LIMIT = 40 * 1024 * 1024

bf16 = jnp.bfloat16
f32 = jnp.float32


def vmem():
    return pl.BlockSpec(memory_space=pltpu.VMEM)


def smem():
    return pl.BlockSpec(memory_space=pltpu.SMEM)


def hbm():
    return pl.BlockSpec(memory_space=pltpu.HBM)


def params():
    return pltpu.CompilerParams(vmem_limit_bytes=VMEM_LIMIT)


def cost(flops, nbytes):
    return pl.CostEstimate(flops=int(flops), bytes_accessed=int(nbytes), transcendentals=0)


def slot_of(column, role, step):
    odd = column % 2
    if role == 0:
        across = 0
    elif role == 1:
        across = 1 - 2 * odd
    else:
        across = 2 * odd - 1
    return 3 * (across + 1) + (step + 1)


def my_column():
    return lax.rem(lax.axis_index("blk"), GY)


def my_row():
    return lax.div(lax.axis_index("blk"), GY)


def step_of(move):
    if move == "swap":
        return 1 - 2 * my_row()
    return -move


def pack_kernel(moves, rt_ref, ct_ref, rs_ref, cs_ref, foot_ref, off_ref, fr_ref, fc_ref, tile_ref, *refs):
    outs, (buf, fbuf, sems) = refs[:-3], refs[-3:]
    ext_ref, packed = outs[0], outs[1:]
    size = tile_ref.shape[0]
    whole = pltpu.make_async_copy(tile_ref, ext_ref.at[pl.ds(0, size)], sems.at[0])
    whole.start()
    edge = fr_ref.shape[1]
    fbuf[...] = jnp.zeros(fbuf.shape, bf16)
    fbuf[0:1, 0:edge] = fr_ref[...]
    fbuf[0:1, edge : 2 * edge] = fc_ref[...]
    tail = pltpu.make_async_copy(fbuf, ext_ref.at[pl.ds(size, EXTRA)], sems.at[1])
    tail.start()
    column = my_column()
    most = (size - BAND) // LANE - 1
    steps = [0] + [step_of(move) for move in moves]
    for group, step in enumerate(steps):
        for role in range(3):
            k = jnp.clip(slot_of(column, role, step), 0, 8)
            used = foot_ref[k].astype(f32)
            buf[0:TAPS] = rt_ref[k].astype(f32)
            buf[TAPS : 2 * TAPS] = ct_ref[k].astype(f32) * used
            for dim, ref in enumerate((rs_ref, cs_ref)):
                off = off_ref[2 * k + dim]
                base = jnp.minimum(lax.div(off, LANE), most)
                rel = ref[pl.ds(k, 1), :] + (off - base * LANE)
                high = lax.shift_right_logical(rel, 5)
                buf[8 + 2 * dim : 9 + 2 * dim] = high.astype(f32)
                buf[9 + 2 * dim : 10 + 2 * dim] = (rel - high * 32).astype(f32)
                buf[12 + dim : 13 + dim] = jnp.zeros((1, edge), f32) + base.astype(f32)
            buf[14:16] = jnp.zeros((2, edge), f32)
            packed[group][role] = buf[...].astype(bf16)
    whole.wait()
    tail.wait()


def pack(moves, rt, ct, rs, cs, foot, off, fr, fc, tile):
    size, edge = tile.shape[0], rs.shape[1]
    groups = 1 + len(moves)
    return pl.pallas_call(
        functools.partial(pack_kernel, moves),
        name="pack",
        out_shape=[jax.ShapeDtypeStruct((size + EXTRA, tile.shape[1]), bf16)]
        + [jax.ShapeDtypeStruct((3, 16, edge), bf16)] * groups,
        in_specs=[vmem()] * 4 + [smem()] * 2 + [vmem()] * 2 + [hbm()],
        out_specs=[hbm()] + [vmem()] * groups,
        scratch_shapes=[
            pltpu.VMEM((16, edge), f32),
            pltpu.VMEM((EXTRA, tile.shape[1]), bf16),
            pltpu.SemaphoreType.DMA((2,)),
        ],
        compiler_params=params(),
        cost_estimate=cost(1e6, 5e6),
    )(rt, ct, rs, cs, foot, off, fr, fc, tile)


def row_matrix(prm, edge):
    cols = prm.T
    rel = cols[:, 8:9] * 32.0 + cols[:, 9:10]
    rel = jnp.broadcast_to(rel, (edge, LANE))
    taps = [jnp.broadcast_to(cols[:, q : q + 1], (edge, LANE)).astype(bf16) for q in range(TAPS)]
    lane = lax.broadcasted_iota(jnp.int32, (edge, LANE), 1).astype(f32)
    parts = []
    for h in range(WIN // LANE):
        place = ((lane + float(LANE * h)) - rel).astype(bf16)
        part = jnp.zeros((edge, LANE), bf16)
        for q in range(TAPS):
            part = jnp.where(place == bf16(q), taps[q], part)
        parts.append(part)
    return jnp.concatenate(parts, axis=1)


def col_matrix(prm, edge):
    rel = prm[10:11] * 32.0 + prm[11:12]
    taps = [jnp.broadcast_to(prm[TAPS + q : TAPS + q + 1], (LANE, edge)).astype(bf16) for q in range(TAPS)]
    sub = lax.broadcasted_iota(jnp.int32, (LANE, edge), 0).astype(f32)
    parts = []
    for h in range(WIN // LANE):
        place = (sub - (rel - float(LANE * h))).astype(bf16)
        part = jnp.zeros((LANE, edge), bf16)
        for q in range(TAPS):
            part = jnp.where(place == bf16(q), taps[q], part)
        parts.append(part)
    return jnp.concatenate(parts, axis=0)


def contrib_kernel(slots, only_middle, feather_row, prm_ref, *refs):
    count = len(slots)
    tiles, out_ref = refs[:count], refs[count]
    win, fth, sems = refs[count + 1 :]
    edge = out_ref.shape[1]
    size = tiles[0].shape[0] - EXTRA

    def work():
        copies = []
        for s, slot in enumerate(slots):
            base = prm_ref[slot].astype(f32)
            r0 = pl.multiple_of(jnp.max(base[12:13, 0:LANE]).astype(jnp.int32) * LANE, LANE)
            c0 = pl.multiple_of(jnp.max(base[13:14, 0:LANE]).astype(jnp.int32) * LANE, LANE)
            window = pltpu.make_async_copy(
                tiles[s].at[pl.ds(r0, WIN), pl.ds(c0, WIN)], win.at[s], sems.at[s, 0]
            )
            feather = pltpu.make_async_copy(tiles[s].at[pl.ds(size, EXTRA)], fth.at[s], sems.at[s, 1])
            window.start()
            feather.start()
            copies.append((window, feather))
        total = None
        profiles = []
        for s, slot in enumerate(slots):
            prm = prm_ref[slot].astype(f32)
            rmat = row_matrix(prm, edge)
            cmat = col_matrix(prm, edge)
            copies[s][0].wait()
            copies[s][1].wait()
            rows = jnp.dot(rmat, win[s], preferred_element_type=f32).astype(bf16)
            contrib = jnp.dot(rows, cmat, preferred_element_type=f32)
            profile = fth[s].astype(f32)
            profiles += [profile[0:1, :edge], profile[0:1, edge:]]
            contrib = contrib * profile[:, :edge].T[:, 0:1] * profile[0:1, edge:]
            total = contrib if total is None else total + contrib
        out_ref[0:edge] = total.astype(out_ref.dtype)
        before = [jnp.zeros((feather_row, edge), f32)] if feather_row else []
        after = [jnp.zeros((EXTRA - feather_row - len(profiles), edge), f32)]
        out_ref[edge:] = jnp.concatenate(before + profiles + after, axis=0).astype(out_ref.dtype)

    if only_middle:
        column = my_column()
        pl.when(jnp.logical_and(column > 0, column < GY - 1))(work)
    else:
        work()


def contributions(name, prm, slots, tiles, edge, only_middle=False, feather_row=0):
    count = len(slots)
    return pl.pallas_call(
        functools.partial(contrib_kernel, slots, only_middle, feather_row),
        name=name,
        out_shape=jax.ShapeDtypeStruct((edge + EXTRA, edge), bf16),
        in_specs=[vmem()] + [hbm()] * count,
        out_specs=vmem(),
        scratch_shapes=[
            pltpu.VMEM((count, WIN, WIN), bf16),
            pltpu.VMEM((count, EXTRA, tiles[0].shape[1]), bf16),
            pltpu.SemaphoreType.DMA((count, 2)),
        ],
        compiler_params=params(),
        cost_estimate=cost(1.0e9 * count * 2, 1.2e6 * count + 5e5),
    )(prm, *tiles)


def weights_of(foot_ref, column, step, rows, roles):
    total = None
    cols = rows.T
    for role in roles:
        slot = slot_of(column, role, step)
        inside = jnp.logical_and(slot >= 0, slot < 9)
        used = jnp.where(inside, foot_ref[jnp.clip(slot, 0, 8)], 0).astype(f32)
        term = cols[:, 2 * role : 2 * role + 1] * (rows[2 * role + 1 : 2 * role + 2] * used)
        total = term if total is None else total + term
    return total


def same_row_kernel(foot_ref, own_ref, cross_ref, numer_ref, denom_ref):
    edge = own_ref.shape[1]
    rows = own_ref[edge:].astype(f32) + cross_ref[edge:].astype(f32)
    numer_ref[...] = own_ref[0:edge].astype(f32) + cross_ref[0:edge].astype(f32)
    denom_ref[...] = weights_of(foot_ref, my_column(), 0, rows, range(3))


def same_row(foot, own, cross, edge):
    return pl.pallas_call(
        same_row_kernel,
        name="same_row",
        out_shape=[jax.ShapeDtypeStruct((edge, edge), f32)] * 2,
        in_specs=[smem(), vmem(), vmem()],
        out_specs=[vmem(), vmem()],
        compiler_params=params(),
        cost_estimate=cost(4e6, 3e6),
    )(foot, own, cross)


def finish_kernel(moves, foot_ref, numer_ref, denom_ref, *refs):
    arrived, (blended_ref, pooled_ref, half) = refs[:-3], refs[-3:]
    edge = numer_ref.shape[0]
    numer, denom = numer_ref[...], denom_ref[...]
    for n, move in enumerate(moves):
        first, second = arrived[2 * n], arrived[2 * n + 1]
        numer = numer + (first[0:edge].astype(f32) + second[0:edge].astype(f32))
        rows = first[edge:].astype(f32) + second[edge:].astype(f32)
        denom = denom + weights_of(foot_ref, my_column(), step_of(move), rows, range(3))
    blended = (numer / denom).astype(bf16)
    blended_ref[...] = blended
    source = lax.broadcasted_iota(jnp.int32, (edge, edge // 2), 0)
    target = lax.broadcasted_iota(jnp.int32, (edge, edge // 2), 1)
    pairs = jnp.where(lax.shift_right_logical(source, 1) == target, 1.0, 0.0).astype(bf16)
    pooled = jnp.dot(blended, pairs, preferred_element_type=f32) * 0.25
    for h in range(edge // 2 // LANE):
        half[h] = pooled[:, h * LANE : (h + 1) * LANE]
        total = half[h, pl.ds(0, edge // 2, stride=2), :] + half[h, pl.ds(1, edge // 2, stride=2), :]
        pooled_ref[:, h * LANE : (h + 1) * LANE] = total.astype(bf16)


def finish(moves, foot, numer, denom, arrived, edge):
    return pl.pallas_call(
        functools.partial(finish_kernel, moves),
        name="finish",
        out_shape=[
            jax.ShapeDtypeStruct((edge, edge), bf16),
            jax.ShapeDtypeStruct((edge // 2, edge // 2), bf16),
        ],
        in_specs=[smem(), vmem(), vmem()] + [vmem()] * len(arrived),
        out_specs=[vmem(), vmem()],
        scratch_shapes=[pltpu.VMEM((edge // 2 // LANE, edge, LANE), f32)],
        compiler_params=params(),
        cost_estimate=cost(3e8, 4e6),
    )(foot, numer, denom, *arrived)


def general_device(
    tiles, row_taps, col_taps, row_starts, col_starts, feather_rows, feather_cols, footprint, offsets
):
    tile = tiles[0, 0]
    edge = row_starts.shape[3]
    devices = lax.axis_size("blk")
    rows = devices // GY
    moves = ["swap"] if rows == 2 else [1, -1]
    foot = footprint.reshape(9)

    def along(move, value, columns=range(GY), back=False):
        pairs = []
        for r in range(rows):
            to = (1 - r) if move == "swap" else r + (-move if back else move)
            if 0 <= to < rows:
                pairs += [(r * GY + c, to * GY + c) for c in columns]
        return lax.ppermute(value, "blk", pairs)

    def mate(value):
        return lax.ppermute(value, "blk", [(i, i ^ 1) for i in range(devices)])

    def cross(value):
        pairs = []
        for r in range(rows):
            for c in range(1, GY - 1, 2):
                pairs += [(r * GY + c, r * GY + c + 1), (r * GY + c + 1, r * GY + c)]
        return lax.ppermute(value, "blk", pairs)

    packed = pack(
        moves,
        row_taps[0, 0],
        col_taps[0, 0],
        row_starts[0, 0],
        col_starts[0, 0],
        foot,
        offsets.reshape(18),
        feather_rows[0],
        feather_cols[0],
        tile,
    )
    ext, own_prm, move_prm = packed[0], packed[1], packed[2:]
    ext_mate = mate(ext)
    asked = [along(move, prm, back=True) for move, prm in zip(moves, move_prm)]
    cross_prm = cross(jnp.stack([own_prm[2]] + [prm[2] for prm in asked]))
    arrived = []
    for n, move in enumerate(moves):
        over = contributions("cross_sum", cross_prm, [1 + n], [ext], edge, True, 4)
        over = cross(over)
        local = contributions("local_sum", asked[n], [0, 1], [ext, ext_mate], edge)
        arrived.append(along(move, local, [0, GY - 1]))
        arrived.append(along(move, local + over, range(1, GY - 1)))
    side = cross(contributions("cross_own", cross_prm, [0], [ext], edge, True, 4))
    own = contributions("local_own", own_prm, [0, 1], [ext, ext_mate], edge)
    numer, denom = same_row(foot, own, side, edge)
    blended, pooled = finish(moves, foot, numer, denom, arrived, edge)
    sections = lax.axis_size("sec")
    before = lax.ppermute(pooled, "sec", [(i, i + 1) for i in range(sections - 1)])
    after = lax.ppermute(pooled, "sec", [(i + 1, i) for i in range(sections - 1)])
    index = lax.axis_index("sec")
    present = 4.0 - (index == 0).astype(f32) - (index == sections - 1).astype(f32)
    level = (before.astype(f32) + 2.0 * pooled.astype(f32) + after.astype(f32)) / present
    return blended[None, None], level.astype(bf16)[None, None]


HALF = 12
PROFILE = 24
BESIDE = 26
SCALARS = 28
CORNER = 8
ROWS = 32
STRIPS = 8
TILE = 1024
PREPARE_VMEM = 40 * 1024 * 1024
WORK_VMEM = 40 * 1024 * 1024


def is_outer():
    column = my_column()
    return jnp.logical_or(column == 0, column == GY - 1)


def prepare_kernel(rt_hbm, ct_hbm, rs_hbm, cs_hbm, foot_hbm, off_hbm, fr_hbm, fc_hbm, tile_hbm, *refs):
    outs, near_ref = refs[:4], refs[4]
    rt_ref, ct_ref, rs_ref, cs_ref, fr_ref, fc_ref, foot_ref, off_ref, buf, sems, tile_sems = refs[5:]
    pairs = [
        (off_hbm, off_ref),
        (foot_hbm, foot_ref),
        (rt_hbm, rt_ref),
        (ct_hbm, ct_ref),
        (rs_hbm, rs_ref),
        (cs_hbm, cs_ref),
        (fr_hbm, fr_ref),
        (fc_hbm, fc_ref),
    ]
    copies = [pltpu.make_async_copy(a, b, sems.at[i]) for i, (a, b) in enumerate(pairs)]
    for copy in copies:
        copy.start()
    strip = near_ref.shape[0] // STRIPS
    strips = []
    for n in range(STRIPS):
        rows = pl.ds(n * strip, strip)
        strips.append(pltpu.make_async_copy(tile_hbm.at[rows], near_ref.at[rows], tile_sems.at[n]))
    for copy in strips:
        copy.start()
    for copy in copies:
        copy.wait()
    edge = fr_ref.shape[1]
    column = my_column()
    over = 1 - 2 * my_row()
    most = (TILE - BAND) // LANE - 1
    lane = lax.broadcasted_iota(jnp.int32, (1, edge), 1)
    scalars = jnp.zeros((1, edge), f32)
    for n in range(6):
        slot = slot_of(column, n % 3, 0 if n < 3 else over)
        inside = jnp.logical_and(slot >= 0, slot < 9)
        used = jnp.where(inside, foot_ref[0, jnp.clip(slot, 0, 8)], 0).astype(f32)
        scalars = jnp.where(lane == n, used, scalars)

    outer = is_outer()

    def message(out_ref, slots, profile_row):
        row = scalars
        buf[...] = jnp.zeros(buf.shape, f32)
        for half, slot in enumerate(slots):
            k = jnp.clip(slot, 0, 8)
            used = foot_ref[0, k].astype(f32)
            at = half * HALF
            buf[at : at + TAPS] = rt_ref[k].astype(f32)
            buf[at + TAPS : at + 2 * TAPS] = ct_ref[k].astype(f32) * used
            for dim, ref in enumerate((rs_ref, cs_ref)):
                off = off_ref[dim, k]
                base = jnp.minimum(lax.div(off, LANE), most)
                rel = ref[k] + (off - base * LANE)
                high = lax.shift_right_logical(rel, 5)
                first = at + 2 * TAPS + 2 * dim
                buf[first : first + 1] = high.astype(f32)
                buf[first + 1 : first + 2] = (rel - high * 32).astype(f32)
                row = jnp.where(lane == CORNER + 2 * half + dim, base.astype(f32), row)
        buf[profile_row : profile_row + 1] = fr_ref[...].astype(f32)
        buf[profile_row + 1 : profile_row + 2] = fc_ref[...].astype(f32)
        buf[SCALARS : SCALARS + 1] = row
        out_ref[...] = buf[...].astype(bf16)

    center, beside, across = (slot_of(column, role, over) for role in range(3))
    message(outs[0], [jnp.where(outer, center, across), beside], PROFILE)
    message(outs[1], [center, beside], PROFILE)
    message(outs[2], [slot_of(column, 2, 0)], BESIDE)
    message(outs[3], [slot_of(column, 0, 0), slot_of(column, 1, 0)], PROFILE)
    for copy in strips:
        copy.wait()


def prepare(rt, ct, rs, cs, foot, off, fr, fc, tile):
    edge = fr.shape[1]
    args = [pltpu.with_memory_space_constraint(x, pltpu.HBM) for x in (rt, ct, rs, cs, foot, off, fr, fc, tile)]
    return pl.pallas_call(
        prepare_kernel,
        name="prepare",
        out_shape=[jax.ShapeDtypeStruct((ROWS, edge), bf16)] * 4 + [jax.ShapeDtypeStruct(tile.shape, bf16)],
        in_specs=[hbm()] * 9,
        out_specs=[vmem()] * 5,
        scratch_shapes=[pltpu.VMEM(x.shape, x.dtype) for x in (rt, ct, rs, cs, fr, fc)]
        + [pltpu.SMEM(x.shape, x.dtype) for x in (foot, off)]
        + [pltpu.VMEM((ROWS, edge), f32), pltpu.SemaphoreType.DMA((8,)), pltpu.SemaphoreType.DMA((STRIPS,))],
        compiler_params=pltpu.CompilerParams(vmem_limit_bytes=PREPARE_VMEM),
        cost_estimate=cost(1e6, 2e5),
    )(*args)


def scalar_of(msg, n):
    lane = lax.broadcasted_iota(jnp.int32, (1, LANE), 1)
    return jnp.sum(jnp.where(lane == n, msg[SCALARS : SCALARS + 1, 0:LANE], 0.0))


def corner(msg, half):
    r0 = pl.multiple_of(scalar_of(msg, CORNER + 2 * half).astype(jnp.int32) * LANE, LANE)
    c0 = pl.multiple_of(scalar_of(msg, CORNER + 2 * half + 1).astype(jnp.int32) * LANE, LANE)
    return pl.ds(r0, WIN), pl.ds(c0, WIN)


def window_copy(msg, half, mate_ref, win, sem):
    copy = pltpu.make_async_copy(mate_ref.at[corner(msg, half)], win, sem)
    copy.start()
    return copy


def contribution(msg, half, profile, tile_ref, edge, copy=None):
    prm = msg[half * HALF : half * HALF + HALF]
    prm = jnp.concatenate([prm, profile, jnp.zeros((2, edge), f32)], axis=0)
    rmat = row_matrix(prm, edge)
    cmat = col_matrix(prm, edge)
    if copy is None:
        window = tile_ref[corner(msg, half)]
    else:
        copy.wait()
        window = tile_ref[...]
    rows = jnp.dot(rmat, window, preferred_element_type=f32).astype(bf16)
    contrib = jnp.dot(rows, cmat, preferred_element_type=f32)
    return contrib * prm.T[:, HALF : HALF + 1] * profile[1:2]


def local_pair(msg, profile, beside, tile_ref, mate_ref, win, sem, edge):
    copy = window_copy(msg, 1, mate_ref, win, sem)
    total = contribution(msg, 0, profile, tile_ref, edge)
    return total + contribution(msg, 1, beside, win, edge, copy)


def weight_sum(msg, profiles):
    edge = msg.shape[1]
    lane = lax.broadcasted_iota(jnp.int32, (1, edge), 1)
    pad = [jnp.zeros((16 - len(profiles), edge), f32)]
    rows, cols = [], []
    for n, profile in enumerate(profiles):
        used = jnp.sum(jnp.where(lane == n, msg[SCALARS : SCALARS + 1], 0.0), axis=1, keepdims=True)
        rows.append(profile[0:1])
        cols.append(profile[1:2] * used)
    rows = jnp.concatenate(rows + pad, axis=0)
    cols = jnp.concatenate(cols + pad, axis=0)
    return jnp.dot(rows.T.astype(bf16), cols.astype(bf16), preferred_element_type=f32)


def pool(block, half):
    edge = block.shape[0]
    source = lax.broadcasted_iota(jnp.int32, (edge, edge // 2), 0)
    target = lax.broadcasted_iota(jnp.int32, (edge, edge // 2), 1)
    pairs = jnp.where(lax.shift_right_logical(source, 1) == target, 0.25, 0.0).astype(bf16)
    sums = jnp.dot(block, pairs, preferred_element_type=f32)
    parts = []
    for h in range(edge // 2 // LANE):
        half[h] = sums[:, h * LANE : (h + 1) * LANE]
        parts.append(half[h, pl.ds(0, edge // 2, stride=2), :] + half[h, pl.ds(1, edge // 2, stride=2), :])
    return jnp.concatenate(parts, axis=1)


def behind(profiles, edge):
    return jnp.concatenate(profiles + [jnp.zeros((EXTRA - 2 * len(profiles), edge), f32)], axis=0).astype(bf16)


def own_profiles(mine_ref, theirs_ref):
    mine, theirs = mine_ref[...].astype(f32), theirs_ref[...].astype(f32)
    return mine[PROFILE : PROFILE + 2], theirs[BESIDE : BESIDE + 2]


def first_kernel(got_ref, mine_ref, theirs_ref, tile_ref, mate_ref, out_ref, win, sem):
    edge = out_ref.shape[1]
    outer = is_outer()
    profile, beside = own_profiles(mine_ref, theirs_ref)
    msg = got_ref[...].astype(f32)

    @pl.when(outer)
    def _():
        total = local_pair(msg, profile, beside, tile_ref, mate_ref, win, sem, edge)
        out_ref[0:edge] = total.astype(bf16)
        out_ref[edge:] = behind([profile, beside], edge)

    @pl.when(jnp.logical_not(outer))
    def _():
        out_ref[0:edge] = contribution(msg, 0, profile, tile_ref, edge).astype(bf16)
        out_ref[edge:] = behind([profile], edge)


def second_kernel(down_ref, mine_ref, theirs_ref, tile_ref, mate_ref, out_ref, win, sem):
    edge = out_ref.shape[1]
    outer = is_outer()
    profile, beside = own_profiles(mine_ref, theirs_ref)
    msg = down_ref[...].astype(f32)

    @pl.when(outer)
    def _():
        copy = window_copy(msg, 0, mate_ref, win, sem)
        out_ref[0:edge] = contribution(msg, 0, beside, win, edge, copy).astype(bf16)
        out_ref[edge:] = behind([beside], edge)

    @pl.when(jnp.logical_not(outer))
    def _():
        total = local_pair(msg, profile, beside, tile_ref, mate_ref, win, sem, edge)
        out_ref[0:edge] = total.astype(bf16)
        out_ref[edge:] = jnp.zeros((EXTRA, edge), bf16)


def merge_kernel(local_ref, over_ref, got_ref, down_ref, mine_ref, theirs_ref, out_ref, pooled_ref, half):
    edge = out_ref.shape[1]

    @pl.when(jnp.logical_not(is_outer()))
    def _():
        profile, beside = own_profiles(mine_ref, theirs_ref)
        msg = down_ref[...].astype(f32)
        across = got_ref[...].astype(f32)[PROFILE : PROFILE + 2]
        theirs = [msg[PROFILE : PROFILE + 2], msg[BESIDE : BESIDE + 2], across]
        denom = weight_sum(msg, theirs + [profile, beside, over_ref[edge:].astype(f32)[0:2]])
        total = local_ref[0:edge].astype(f32) + over_ref[0:edge].astype(f32)
        block = (total / denom).astype(bf16)
        out_ref[...] = block
        pooled_ref[...] = pool(block, half).astype(bf16)


def own_kernel(own_ref, mine_ref, theirs_ref, tile_ref, mate_ref, out_ref, win, sem):
    profile, beside = own_profiles(mine_ref, theirs_ref)
    msg = own_ref[...].astype(f32)
    out_ref[...] = local_pair(msg, profile, beside, tile_ref, mate_ref, win, sem, out_ref.shape[1])


def blend_kernel(
    local_ref, side_ref, got_ref, down_ref, mine_ref, theirs_ref, early_ref, pooled_early_ref, out_ref, pooled_ref, half
):
    edge = out_ref.shape[1]
    outer = is_outer()
    profile, beside = own_profiles(mine_ref, theirs_ref)
    got, down = got_ref[...].astype(f32), down_ref[...].astype(f32)
    rows = early_ref[edge:].astype(f32)
    opposite = jnp.where(outer, rows[0:2], down[PROFILE : PROFILE + 2])
    opposite_beside = jnp.where(outer, rows[2:4], down[BESIDE : BESIDE + 2])
    theirs = [opposite, opposite_beside, got[PROFILE : PROFILE + 2]]
    mine_across = side_ref[edge:].astype(f32)[0:2]
    denom = weight_sum(mine_ref[...].astype(f32), [profile, beside, mine_across] + theirs)
    early = jnp.where(outer, early_ref[0:edge].astype(f32), 0.0)
    block = (local_ref[...] + side_ref[0:edge].astype(f32) + early) / denom
    out_ref[...] = block
    pooled_ref[...] = (pool(block.astype(bf16), half) + pooled_early_ref[...].astype(f32)).astype(bf16)


def last_kernel(block_ref, late_ref, out_ref):
    out_ref[...] = (block_ref[...] + late_ref[...].astype(f32)).astype(bf16)


def call(kernel, name, out_shape, operands, mate=None, halves=False, work=(1e9, 4e6)):
    single = not isinstance(out_shape, list)
    edge = (out_shape if single else out_shape[0]).shape[1]
    scratch, far = [], []
    if mate is not None:
        scratch = [pltpu.VMEM((WIN, WIN), bf16), pltpu.SemaphoreType.DMA]
        far = [pltpu.with_memory_space_constraint(mate, pltpu.HBM)]
    if halves:
        scratch = [pltpu.VMEM((edge // 2 // LANE, edge, LANE), f32)]
    return pl.pallas_call(
        kernel,
        name=name,
        out_shape=out_shape,
        in_specs=[vmem()] * len(operands) + [hbm()] * len(far),
        out_specs=vmem() if single else [vmem()] * len(out_shape),
        scratch_shapes=scratch,
        compiler_params=pltpu.CompilerParams(vmem_limit_bytes=WORK_VMEM),
        cost_estimate=cost(*work),
    )(*[pltpu.with_memory_space_constraint(x, pltpu.VMEM) for x in operands], *far)


def two_row_device(
    tiles, row_taps, col_taps, row_starts, col_starts, feather_rows, feather_cols, footprint, offsets
):
    tile = tiles[0, 0]
    edge = row_starts.shape[3]
    devices = lax.axis_size("blk")

    def send(value, pairs):
        return lax.ppermute(value, "blk", pairs)

    def swap(pairs):
        return [(i, j) for i, j in pairs] + [(j, i) for i, j in pairs]

    in_chip = [(i, i ^ 1) for i in range(devices)]
    vertical_outer = swap([(0, 4), (3, 7)])
    vertical_inner = swap([(1, 5), (2, 6)])
    diagonal = swap([(1, 6), (2, 5)])
    across_inner = swap([(1, 2), (5, 6)])
    across_outer = swap([(0, 3), (4, 7)])
    outer_to_inner = [(0, 2), (3, 1), (4, 6), (7, 5)]

    asked, mine, aside, own_msg, near = prepare(
        row_taps[0, 0],
        col_taps[0, 0],
        row_starts.reshape(-1, 1, edge),
        col_starts.reshape(-1, 1, edge),
        footprint[0],
        offsets[0, 0].T,
        feather_rows[0],
        feather_cols[0],
        tile,
    )
    mate = send(tile, in_chip)
    outer = is_outer()
    got = send(asked, vertical_outer + diagonal)
    theirs = send(aside, in_chip)
    row = lax.broadcasted_iota(jnp.int32, mine.shape, 0)
    from_beside = jnp.logical_and(row >= BESIDE, row < BESIDE + 2)
    asking = jnp.where(from_beside, theirs, mine)
    down = send(jnp.where(outer, theirs, asking), across_outer + vertical_inner)

    block = jax.ShapeDtypeStruct((edge + EXTRA, edge), bf16)
    bare = jax.ShapeDtypeStruct((edge, edge), bf16)
    bare32 = jax.ShapeDtypeStruct((edge, edge), f32)
    pooled = jax.ShapeDtypeStruct((edge // 2, edge // 2), bf16)
    two = (4e9, 4e6)
    tiny = (1e4, 1e4)

    first = call(first_kernel, "first", block, (got, mine, theirs, near), mate, work=tiny)
    early = send(first, vertical_outer + across_inner)
    down, first = lax.optimization_barrier((down, first))
    second = call(second_kernel, "second", block, (down, mine, theirs, near), mate, work=two)
    own_msg, second = lax.optimization_barrier((own_msg, second))
    local = call(own_kernel, "own", bare32, (own_msg, mine, theirs, near), mate, work=two)
    second, local = lax.optimization_barrier((second, local))
    side = send(second, outer_to_inner)
    early, local = lax.optimization_barrier((early, local))
    late_out, pooled_out = call(
        merge_kernel, "merge", [bare, pooled], (second, early, got, down, mine, theirs), halves=True
    )
    pooled_late = send(pooled_out, vertical_inner)
    late = send(late_out, vertical_inner)
    block_so_far, pooled_all = call(
        blend_kernel,
        "blend",
        [bare32, pooled],
        (local, side, got, down, mine, theirs, early, pooled_late),
        halves=True,
    )
    sections = lax.axis_size("sec")
    before = lax.ppermute(pooled_all, "sec", [(i, i + 1) for i in range(sections - 1)])
    after = lax.ppermute(pooled_all, "sec", [(i + 1, i) for i in range(sections - 1)])
    blended = call(last_kernel, "last", bare, (block_so_far, late), work=(1e6, 2e6))
    index = lax.axis_index("sec")
    present = 4.0 - (index == 0).astype(f32) - (index == sections - 1).astype(f32)
    level = (before.astype(f32) + 2.0 * pooled_all.astype(f32) + after.astype(f32)) / present
    return blended[None, None], level.astype(bf16)[None, None]


def per_device(*args):
    if lax.axis_size("blk") == 2 * GY:
        return two_row_device(*args)
    return general_device(*args)


def solution(mesh):
    return jax.shard_map(
        per_device,
        mesh=mesh,
        in_specs=(
            P("sec", "blk", None, None),
            P("sec", "blk", None, None, None),
            P("sec", "blk", None, None, None),
            P("sec", "blk", None, None),
            P("sec", "blk", None, None),
            P("sec", "blk", None),
            P("sec", "blk", None),
            P("sec", "blk", None),
            P("sec", "blk", None, None),
        ),
        out_specs=(P("sec", "blk", None, None), P("sec", "blk", None, None)),
        check_vma=False,
    )
```

```python
import functools

import jax
import jax.numpy as jnp
from jax import lax
from jax.experimental import pallas as pl
from jax.experimental.pallas import tpu as pltpu
from jax.sharding import PartitionSpec as P

BAND = 640
GY = 4
TAPS = 4
LANE = 128
WIN = BAND + LANE
EXTRA = 16
VMEM_LIMIT = 40 * 1024 * 1024

bf16 = jnp.bfloat16
f32 = jnp.float32


def vmem():
    return pl.BlockSpec(memory_space=pltpu.VMEM)


def smem():
    return pl.BlockSpec(memory_space=pltpu.SMEM)


def hbm():
    return pl.BlockSpec(memory_space=pltpu.HBM)


def params():
    return pltpu.CompilerParams(vmem_limit_bytes=VMEM_LIMIT)


def cost(flops, nbytes):
    return pl.CostEstimate(flops=int(flops), bytes_accessed=int(nbytes), transcendentals=0)


def slot_of(column, role, step):
    odd = column % 2
    if role == 0:
        across = 0
    elif role == 1:
        across = 1 - 2 * odd
    else:
        across = 2 * odd - 1
    return 3 * (across + 1) + (step + 1)


def my_column():
    return lax.rem(lax.axis_index("blk"), GY)


def my_row():
    return lax.div(lax.axis_index("blk"), GY)


def step_of(move):
    if move == "swap":
        return 1 - 2 * my_row()
    return -move


def pack_kernel(moves, rt_ref, ct_ref, rs_ref, cs_ref, foot_ref, off_ref, fr_ref, fc_ref, tile_ref, *refs):
    outs, (buf, fbuf, sems) = refs[:-3], refs[-3:]
    ext_ref, packed = outs[0], outs[1:]
    size = tile_ref.shape[0]
    whole = pltpu.make_async_copy(tile_ref, ext_ref.at[pl.ds(0, size)], sems.at[0])
    whole.start()
    edge = fr_ref.shape[1]
    fbuf[...] = jnp.zeros(fbuf.shape, bf16)
    fbuf[0:1, 0:edge] = fr_ref[...]
    fbuf[0:1, edge : 2 * edge] = fc_ref[...]
    tail = pltpu.make_async_copy(fbuf, ext_ref.at[pl.ds(size, EXTRA)], sems.at[1])
    tail.start()
    column = my_column()
    most = (size - BAND) // LANE - 1
    steps = [0] + [step_of(move) for move in moves]
    for group, step in enumerate(steps):
        for role in range(3):
            k = jnp.clip(slot_of(column, role, step), 0, 8)
            used = foot_ref[k].astype(f32)
            buf[0:TAPS] = rt_ref[k].astype(f32)
            buf[TAPS : 2 * TAPS] = ct_ref[k].astype(f32) * used
            for dim, ref in enumerate((rs_ref, cs_ref)):
                off = off_ref[2 * k + dim]
                base = jnp.minimum(lax.div(off, LANE), most)
                rel = ref[pl.ds(k, 1), :] + (off - base * LANE)
                high = lax.shift_right_logical(rel, 5)
                buf[8 + 2 * dim : 9 + 2 * dim] = high.astype(f32)
                buf[9 + 2 * dim : 10 + 2 * dim] = (rel - high * 32).astype(f32)
                buf[12 + dim : 13 + dim] = jnp.zeros((1, edge), f32) + base.astype(f32)
            buf[14:16] = jnp.zeros((2, edge), f32)
            packed[group][role] = buf[...].astype(bf16)
    whole.wait()
    tail.wait()


def pack(moves, rt, ct, rs, cs, foot, off, fr, fc, tile):
    size, edge = tile.shape[0], rs.shape[1]
    groups = 1 + len(moves)
    return pl.pallas_call(
        functools.partial(pack_kernel, moves),
        name="pack",
        out_shape=[jax.ShapeDtypeStruct((size + EXTRA, tile.shape[1]), bf16)]
        + [jax.ShapeDtypeStruct((3, 16, edge), bf16)] * groups,
        in_specs=[vmem()] * 4 + [smem()] * 2 + [vmem()] * 2 + [hbm()],
        out_specs=[hbm()] + [vmem()] * groups,
        scratch_shapes=[
            pltpu.VMEM((16, edge), f32),
            pltpu.VMEM((EXTRA, tile.shape[1]), bf16),
            pltpu.SemaphoreType.DMA((2,)),
        ],
        compiler_params=params(),
        cost_estimate=cost(1e6, 5e6),
    )(rt, ct, rs, cs, foot, off, fr, fc, tile)


def row_matrix(prm, edge):
    cols = prm.T
    rel = cols[:, 8:9] * 32.0 + cols[:, 9:10]
    rel = jnp.broadcast_to(rel, (edge, LANE))
    taps = [jnp.broadcast_to(cols[:, q : q + 1], (edge, LANE)).astype(bf16) for q in range(TAPS)]
    lane = lax.broadcasted_iota(jnp.int32, (edge, LANE), 1).astype(f32)
    parts = []
    for h in range(WIN // LANE):
        place = ((lane + float(LANE * h)) - rel).astype(bf16)
        part = jnp.zeros((edge, LANE), bf16)
        for q in range(TAPS):
            part = jnp.where(place == bf16(q), taps[q], part)
        parts.append(part)
    return jnp.concatenate(parts, axis=1)


def col_matrix(prm, edge):
    rel = prm[10:11] * 32.0 + prm[11:12]
    taps = [jnp.broadcast_to(prm[TAPS + q : TAPS + q + 1], (LANE, edge)).astype(bf16) for q in range(TAPS)]
    sub = lax.broadcasted_iota(jnp.int32, (LANE, edge), 0).astype(f32)
    parts = []
    for h in range(WIN // LANE):
        place = (sub - (rel - float(LANE * h))).astype(bf16)
        part = jnp.zeros((LANE, edge), bf16)
        for q in range(TAPS):
            part = jnp.where(place == bf16(q), taps[q], part)
        parts.append(part)
    return jnp.concatenate(parts, axis=0)


def contrib_kernel(slots, only_middle, feather_row, prm_ref, *refs):
    count = len(slots)
    tiles, out_ref = refs[:count], refs[count]
    win, fth, sems = refs[count + 1 :]
    edge = out_ref.shape[1]
    size = tiles[0].shape[0] - EXTRA

    def work():
        copies = []
        for s, slot in enumerate(slots):
            base = prm_ref[slot].astype(f32)
            r0 = pl.multiple_of(jnp.max(base[12:13, 0:LANE]).astype(jnp.int32) * LANE, LANE)
            c0 = pl.multiple_of(jnp.max(base[13:14, 0:LANE]).astype(jnp.int32) * LANE, LANE)
            window = pltpu.make_async_copy(
                tiles[s].at[pl.ds(r0, WIN), pl.ds(c0, WIN)], win.at[s], sems.at[s, 0]
            )
            feather = pltpu.make_async_copy(tiles[s].at[pl.ds(size, EXTRA)], fth.at[s], sems.at[s, 1])
            window.start()
            feather.start()
            copies.append((window, feather))
        total = None
        profiles = []
        for s, slot in enumerate(slots):
            prm = prm_ref[slot].astype(f32)
            rmat = row_matrix(prm, edge)
            cmat = col_matrix(prm, edge)
            copies[s][0].wait()
            copies[s][1].wait()
            rows = jnp.dot(rmat, win[s], preferred_element_type=f32).astype(bf16)
            contrib = jnp.dot(rows, cmat, preferred_element_type=f32)
            profile = fth[s].astype(f32)
            profiles += [profile[0:1, :edge], profile[0:1, edge:]]
            contrib = contrib * profile[:, :edge].T[:, 0:1] * profile[0:1, edge:]
            total = contrib if total is None else total + contrib
        out_ref[0:edge] = total.astype(out_ref.dtype)
        before = [jnp.zeros((feather_row, edge), f32)] if feather_row else []
        after = [jnp.zeros((EXTRA - feather_row - len(profiles), edge), f32)]
        out_ref[edge:] = jnp.concatenate(before + profiles + after, axis=0).astype(out_ref.dtype)

    if only_middle:
        column = my_column()
        pl.when(jnp.logical_and(column > 0, column < GY - 1))(work)
    else:
        work()


def contributions(name, prm, slots, tiles, edge, only_middle=False, feather_row=0):
    count = len(slots)
    return pl.pallas_call(
        functools.partial(contrib_kernel, slots, only_middle, feather_row),
        name=name,
        out_shape=jax.ShapeDtypeStruct((edge + EXTRA, edge), bf16),
        in_specs=[vmem()] + [hbm()] * count,
        out_specs=vmem(),
        scratch_shapes=[
            pltpu.VMEM((count, WIN, WIN), bf16),
            pltpu.VMEM((count, EXTRA, tiles[0].shape[1]), bf16),
            pltpu.SemaphoreType.DMA((count, 2)),
        ],
        compiler_params=params(),
        cost_estimate=cost(1.0e9 * count * 2, 1.2e6 * count + 5e5),
    )(prm, *tiles)


def weights_of(foot_ref, column, step, rows, roles):
    total = None
    cols = rows.T
    for role in roles:
        slot = slot_of(column, role, step)
        inside = jnp.logical_and(slot >= 0, slot < 9)
        used = jnp.where(inside, foot_ref[jnp.clip(slot, 0, 8)], 0).astype(f32)
        term = cols[:, 2 * role : 2 * role + 1] * (rows[2 * role + 1 : 2 * role + 2] * used)
        total = term if total is None else total + term
    return total


def same_row_kernel(foot_ref, own_ref, cross_ref, numer_ref, denom_ref):
    edge = own_ref.shape[1]
    rows = own_ref[edge:].astype(f32) + cross_ref[edge:].astype(f32)
    numer_ref[...] = own_ref[0:edge].astype(f32) + cross_ref[0:edge].astype(f32)
    denom_ref[...] = weights_of(foot_ref, my_column(), 0, rows, range(3))


def same_row(foot, own, cross, edge):
    return pl.pallas_call(
        same_row_kernel,
        name="same_row",
        out_shape=[jax.ShapeDtypeStruct((edge, edge), f32)] * 2,
        in_specs=[smem(), vmem(), vmem()],
        out_specs=[vmem(), vmem()],
        compiler_params=params(),
        cost_estimate=cost(4e6, 3e6),
    )(foot, own, cross)


def finish_kernel(moves, foot_ref, numer_ref, denom_ref, *refs):
    arrived, (blended_ref, pooled_ref, half) = refs[:-3], refs[-3:]
    edge = numer_ref.shape[0]
    numer, denom = numer_ref[...], denom_ref[...]
    for n, move in enumerate(moves):
        first, second = arrived[2 * n], arrived[2 * n + 1]
        numer = numer + (first[0:edge].astype(f32) + second[0:edge].astype(f32))
        rows = first[edge:].astype(f32) + second[edge:].astype(f32)
        denom = denom + weights_of(foot_ref, my_column(), step_of(move), rows, range(3))
    blended = (numer / denom).astype(bf16)
    blended_ref[...] = blended
    source = lax.broadcasted_iota(jnp.int32, (edge, edge // 2), 0)
    target = lax.broadcasted_iota(jnp.int32, (edge, edge // 2), 1)
    pairs = jnp.where(lax.shift_right_logical(source, 1) == target, 1.0, 0.0).astype(bf16)
    pooled = jnp.dot(blended, pairs, preferred_element_type=f32) * 0.25
    for h in range(edge // 2 // LANE):
        half[h] = pooled[:, h * LANE : (h + 1) * LANE]
        total = half[h, pl.ds(0, edge // 2, stride=2), :] + half[h, pl.ds(1, edge // 2, stride=2), :]
        pooled_ref[:, h * LANE : (h + 1) * LANE] = total.astype(bf16)


def finish(moves, foot, numer, denom, arrived, edge):
    return pl.pallas_call(
        functools.partial(finish_kernel, moves),
        name="finish",
        out_shape=[
            jax.ShapeDtypeStruct((edge, edge), bf16),
            jax.ShapeDtypeStruct((edge // 2, edge // 2), bf16),
        ],
        in_specs=[smem(), vmem(), vmem()] + [vmem()] * len(arrived),
        out_specs=[vmem(), vmem()],
        scratch_shapes=[pltpu.VMEM((edge // 2 // LANE, edge, LANE), f32)],
        compiler_params=params(),
        cost_estimate=cost(3e8, 4e6),
    )(foot, numer, denom, *arrived)


def general_device(
    tiles, row_taps, col_taps, row_starts, col_starts, feather_rows, feather_cols, footprint, offsets
):
    tile = tiles[0, 0]
    edge = row_starts.shape[3]
    devices = lax.axis_size("blk")
    rows = devices // GY
    moves = ["swap"] if rows == 2 else [1, -1]
    foot = footprint.reshape(9)

    def along(move, value, columns=range(GY), back=False):
        pairs = []
        for r in range(rows):
            to = (1 - r) if move == "swap" else r + (-move if back else move)
            if 0 <= to < rows:
                pairs += [(r * GY + c, to * GY + c) for c in columns]
        return lax.ppermute(value, "blk", pairs)

    def mate(value):
        return lax.ppermute(value, "blk", [(i, i ^ 1) for i in range(devices)])

    def cross(value):
        pairs = []
        for r in range(rows):
            for c in range(1, GY - 1, 2):
                pairs += [(r * GY + c, r * GY + c + 1), (r * GY + c + 1, r * GY + c)]
        return lax.ppermute(value, "blk", pairs)

    packed = pack(
        moves,
        row_taps[0, 0],
        col_taps[0, 0],
        row_starts[0, 0],
        col_starts[0, 0],
        foot,
        offsets.reshape(18),
        feather_rows[0],
        feather_cols[0],
        tile,
    )
    ext, own_prm, move_prm = packed[0], packed[1], packed[2:]
    ext_mate = mate(ext)
    asked = [along(move, prm, back=True) for move, prm in zip(moves, move_prm)]
    cross_prm = cross(jnp.stack([own_prm[2]] + [prm[2] for prm in asked]))
    arrived = []
    for n, move in enumerate(moves):
        over = contributions("cross_sum", cross_prm, [1 + n], [ext], edge, True, 4)
        over = cross(over)
        local = contributions("local_sum", asked[n], [0, 1], [ext, ext_mate], edge)
        arrived.append(along(move, local, [0, GY - 1]))
        arrived.append(along(move, local + over, range(1, GY - 1)))
    side = cross(contributions("cross_own", cross_prm, [0], [ext], edge, True, 4))
    own = contributions("local_own", own_prm, [0, 1], [ext, ext_mate], edge)
    numer, denom = same_row(foot, own, side, edge)
    blended, pooled = finish(moves, foot, numer, denom, arrived, edge)
    sections = lax.axis_size("sec")
    before = lax.ppermute(pooled, "sec", [(i, i + 1) for i in range(sections - 1)])
    after = lax.ppermute(pooled, "sec", [(i + 1, i) for i in range(sections - 1)])
    index = lax.axis_index("sec")
    present = 4.0 - (index == 0).astype(f32) - (index == sections - 1).astype(f32)
    level = (before.astype(f32) + 2.0 * pooled.astype(f32) + after.astype(f32)) / present
    return blended[None, None], level.astype(bf16)[None, None]


HALF = 12
PROFILE = 24
BESIDE = 26
SCALARS = 28
CORNER = 8
ROWS = 32
STRIPS = 8
TILE = 1024
PREPARE_VMEM = 40 * 1024 * 1024
WORK_VMEM = 40 * 1024 * 1024


def is_outer():
    column = my_column()
    return jnp.logical_or(column == 0, column == GY - 1)


def prepare_kernel(rt_hbm, ct_hbm, rs_hbm, cs_hbm, foot_hbm, off_hbm, fr_hbm, fc_hbm, tile_hbm, *refs):
    outs, near_ref = refs[:4], refs[4]
    rt_ref, ct_ref, rs_ref, cs_ref, fr_ref, fc_ref, foot_ref, off_ref, buf, sems, tile_sems = refs[5:]
    pairs = [
        (off_hbm, off_ref),
        (foot_hbm, foot_ref),
        (rt_hbm, rt_ref),
        (ct_hbm, ct_ref),
        (rs_hbm, rs_ref),
        (cs_hbm, cs_ref),
        (fr_hbm, fr_ref),
        (fc_hbm, fc_ref),
    ]
    copies = [pltpu.make_async_copy(a, b, sems.at[i]) for i, (a, b) in enumerate(pairs)]
    for copy in copies:
        copy.start()
    strip = near_ref.shape[0] // STRIPS
    strips = []
    for n in range(STRIPS):
        rows = pl.ds(n * strip, strip)
        strips.append(pltpu.make_async_copy(tile_hbm.at[rows], near_ref.at[rows], tile_sems.at[n]))
    for copy in strips:
        copy.start()
    for copy in copies:
        copy.wait()
    edge = fr_ref.shape[1]
    column = my_column()
    over = 1 - 2 * my_row()
    most = (TILE - BAND) // LANE - 1
    lane = lax.broadcasted_iota(jnp.int32, (1, edge), 1)
    scalars = jnp.zeros((1, edge), f32)
    for n in range(6):
        slot = slot_of(column, n % 3, 0 if n < 3 else over)
        inside = jnp.logical_and(slot >= 0, slot < 9)
        used = jnp.where(inside, foot_ref[0, jnp.clip(slot, 0, 8)], 0).astype(f32)
        scalars = jnp.where(lane == n, used, scalars)

    outer = is_outer()

    def message(out_ref, slots, profile_row):
        row = scalars
        buf[...] = jnp.zeros(buf.shape, f32)
        for half, slot in enumerate(slots):
            k = jnp.clip(slot, 0, 8)
            used = foot_ref[0, k].astype(f32)
            at = half * HALF
            buf[at : at + TAPS] = rt_ref[k].astype(f32)
            buf[at + TAPS : at + 2 * TAPS] = ct_ref[k].astype(f32) * used
            for dim, ref in enumerate((rs_ref, cs_ref)):
                off = off_ref[dim, k]
                base = jnp.minimum(lax.div(off, LANE), most)
                rel = ref[k] + (off - base * LANE)
                high = lax.shift_right_logical(rel, 5)
                first = at + 2 * TAPS + 2 * dim
                buf[first : first + 1] = high.astype(f32)
                buf[first + 1 : first + 2] = (rel - high * 32).astype(f32)
                row = jnp.where(lane == CORNER + 2 * half + dim, base.astype(f32), row)
        buf[profile_row : profile_row + 1] = fr_ref[...].astype(f32)
        buf[profile_row + 1 : profile_row + 2] = fc_ref[...].astype(f32)
        buf[SCALARS : SCALARS + 1] = row
        out_ref[...] = buf[...].astype(bf16)

    center, beside, across = (slot_of(column, role, over) for role in range(3))
    message(outs[0], [jnp.where(outer, center, across), beside], PROFILE)
    message(outs[1], [center, beside], PROFILE)
    message(outs[2], [slot_of(column, 2, 0)], BESIDE)
    message(outs[3], [slot_of(column, 0, 0), slot_of(column, 1, 0)], PROFILE)
    for copy in strips:
        copy.wait()


def prepare(rt, ct, rs, cs, foot, off, fr, fc, tile):
    edge = fr.shape[1]
    args = [pltpu.with_memory_space_constraint(x, pltpu.HBM) for x in (rt, ct, rs, cs, foot, off, fr, fc, tile)]
    return pl.pallas_call(
        prepare_kernel,
        name="prepare",
        out_shape=[jax.ShapeDtypeStruct((ROWS, edge), bf16)] * 4 + [jax.ShapeDtypeStruct(tile.shape, bf16)],
        in_specs=[hbm()] * 9,
        out_specs=[vmem()] * 5,
        scratch_shapes=[pltpu.VMEM(x.shape, x.dtype) for x in (rt, ct, rs, cs, fr, fc)]
        + [pltpu.SMEM(x.shape, x.dtype) for x in (foot, off)]
        + [pltpu.VMEM((ROWS, edge), f32), pltpu.SemaphoreType.DMA((8,)), pltpu.SemaphoreType.DMA((STRIPS,))],
        compiler_params=pltpu.CompilerParams(vmem_limit_bytes=PREPARE_VMEM),
        cost_estimate=cost(1e6, 2e5),
    )(*args)


def scalar_of(msg, n):
    lane = lax.broadcasted_iota(jnp.int32, (1, LANE), 1)
    return jnp.sum(jnp.where(lane == n, msg[SCALARS : SCALARS + 1, 0:LANE], 0.0))


def corner(msg, half):
    r0 = pl.multiple_of(scalar_of(msg, CORNER + 2 * half).astype(jnp.int32) * LANE, LANE)
    c0 = pl.multiple_of(scalar_of(msg, CORNER + 2 * half + 1).astype(jnp.int32) * LANE, LANE)
    return pl.ds(r0, WIN), pl.ds(c0, WIN)


def window_copy(msg, half, mate_ref, win, sem):
    copy = pltpu.make_async_copy(mate_ref.at[corner(msg, half)], win, sem)
    copy.start()
    return copy


def contribution(msg, half, profile, tile_ref, edge, copy=None, parts=1):
    prm = msg[half * HALF : half * HALF + HALF]
    prm = jnp.concatenate([prm, profile, jnp.zeros((2, edge), f32)], axis=0)
    rmat = row_matrix(prm, edge)
    cmat = col_matrix(prm, edge)
    if copy is None:
        window = tile_ref[corner(msg, half)]
    else:
        copy.wait()
        window = tile_ref[...]
    weight = prm.T[:, HALF : HALF + 1]
    total = []
    for n in range(parts):
        part = slice(n * edge // parts, (n + 1) * edge // parts)
        rows = jnp.dot(rmat[part], window, preferred_element_type=f32).astype(bf16)
        contrib = jnp.dot(rows, cmat, preferred_element_type=f32)
        total.append(contrib * weight[part] * profile[1:2])
    return jnp.concatenate(total, axis=0) if parts > 1 else total[0]


def local_pair(msg, profile, beside, tile_ref, mate_ref, win, sem, edge, parts=1):
    copy = window_copy(msg, 1, mate_ref, win, sem)
    total = contribution(msg, 0, profile, tile_ref, edge, None, parts)
    return total + contribution(msg, 1, beside, win, edge, copy, parts)


def weight_sum(msg, profiles):
    edge = msg.shape[1]
    lane = lax.broadcasted_iota(jnp.int32, (1, edge), 1)
    pad = [jnp.zeros((16 - len(profiles), edge), f32)]
    rows, cols = [], []
    for n, profile in enumerate(profiles):
        used = jnp.sum(jnp.where(lane == n, msg[SCALARS : SCALARS + 1], 0.0), axis=1, keepdims=True)
        rows.append(profile[0:1])
        cols.append(profile[1:2] * used)
    rows = jnp.concatenate(rows + pad, axis=0)
    cols = jnp.concatenate(cols + pad, axis=0)
    return jnp.dot(rows.T.astype(bf16), cols.astype(bf16), preferred_element_type=f32)


def pool(block, half):
    edge = block.shape[0]
    source = lax.broadcasted_iota(jnp.int32, (edge, edge // 2), 0)
    target = lax.broadcasted_iota(jnp.int32, (edge, edge // 2), 1)
    pairs = jnp.where(lax.shift_right_logical(source, 1) == target, 0.25, 0.0).astype(bf16)
    sums = jnp.dot(block, pairs, preferred_element_type=f32)
    parts = []
    for h in range(edge // 2 // LANE):
        half[h] = sums[:, h * LANE : (h + 1) * LANE]
        parts.append(half[h, pl.ds(0, edge // 2, stride=2), :] + half[h, pl.ds(1, edge // 2, stride=2), :])
    return jnp.concatenate(parts, axis=1)


def behind(profiles, edge):
    return jnp.concatenate(profiles + [jnp.zeros((EXTRA - 2 * len(profiles), edge), f32)], axis=0).astype(bf16)


def own_profiles(mine_ref, theirs_ref):
    mine, theirs = mine_ref[...].astype(f32), theirs_ref[...].astype(f32)
    return mine[PROFILE : PROFILE + 2], theirs[BESIDE : BESIDE + 2]


def first_kernel(got_ref, mine_ref, theirs_ref, tile_ref, mate_ref, out_ref, win, sem):
    edge = out_ref.shape[1]
    outer = is_outer()
    profile, beside = own_profiles(mine_ref, theirs_ref)
    msg = got_ref[...].astype(f32)

    @pl.when(outer)
    def _():
        total = local_pair(msg, profile, beside, tile_ref, mate_ref, win, sem, edge, 2)
        out_ref[0:edge] = total.astype(bf16)
        out_ref[edge:] = behind([profile, beside], edge)

    @pl.when(jnp.logical_not(outer))
    def _():
        out_ref[0:edge] = contribution(msg, 0, profile, tile_ref, edge).astype(bf16)
        out_ref[edge:] = behind([profile], edge)


def second_kernel(down_ref, mine_ref, theirs_ref, tile_ref, mate_ref, out_ref, win, sem):
    edge = out_ref.shape[1]
    outer = is_outer()
    profile, beside = own_profiles(mine_ref, theirs_ref)
    msg = down_ref[...].astype(f32)

    @pl.when(outer)
    def _():
        copy = window_copy(msg, 0, mate_ref, win, sem)
        out_ref[0:edge] = contribution(msg, 0, beside, win, edge, copy).astype(bf16)
        out_ref[edge:] = behind([beside], edge)

    @pl.when(jnp.logical_not(outer))
    def _():
        total = local_pair(msg, profile, beside, tile_ref, mate_ref, win, sem, edge, 4)
        out_ref[0:edge] = total.astype(bf16)
        out_ref[edge:] = jnp.zeros((EXTRA, edge), bf16)


def merge_kernel(local_ref, over_ref, got_ref, down_ref, mine_ref, theirs_ref, out_ref, pooled_ref, half):
    edge = out_ref.shape[1]

    @pl.when(jnp.logical_not(is_outer()))
    def _():
        profile, beside = own_profiles(mine_ref, theirs_ref)
        msg = down_ref[...].astype(f32)
        across = got_ref[...].astype(f32)[PROFILE : PROFILE + 2]
        theirs = [msg[PROFILE : PROFILE + 2], msg[BESIDE : BESIDE + 2], across]
        denom = weight_sum(msg, theirs + [profile, beside, over_ref[edge:].astype(f32)[0:2]])
        total = local_ref[0:edge].astype(f32) + over_ref[0:edge].astype(f32)
        block = (total / denom).astype(bf16)
        out_ref[...] = block
        pooled_ref[...] = pool(block, half).astype(bf16)


def own_kernel(own_ref, mine_ref, theirs_ref, tile_ref, mate_ref, out_ref, win, sem):
    profile, beside = own_profiles(mine_ref, theirs_ref)
    msg = own_ref[...].astype(f32)
    out_ref[...] = local_pair(msg, profile, beside, tile_ref, mate_ref, win, sem, out_ref.shape[1], 4)


def blend_kernel(
    local_ref, side_ref, got_ref, down_ref, mine_ref, theirs_ref, early_ref, pooled_early_ref, out_ref, pooled_ref, half
):
    edge = out_ref.shape[1]
    outer = is_outer()
    profile, beside = own_profiles(mine_ref, theirs_ref)
    got, down = got_ref[...].astype(f32), down_ref[...].astype(f32)
    rows = early_ref[edge:].astype(f32)
    opposite = jnp.where(outer, rows[0:2], down[PROFILE : PROFILE + 2])
    opposite_beside = jnp.where(outer, rows[2:4], down[BESIDE : BESIDE + 2])
    theirs = [opposite, opposite_beside, got[PROFILE : PROFILE + 2]]
    mine_across = side_ref[edge:].astype(f32)[0:2]
    denom = weight_sum(mine_ref[...].astype(f32), [profile, beside, mine_across] + theirs)
    early = jnp.where(outer, early_ref[0:edge].astype(f32), 0.0)
    block = (local_ref[...] + side_ref[0:edge].astype(f32) + early) / denom
    out_ref[...] = block
    pooled_ref[...] = (pool(block.astype(bf16), half) + pooled_early_ref[...].astype(f32)).astype(bf16)


def last_kernel(block_ref, late_ref, before_ref, after_ref, pooled_ref, out_hbm, level_hbm, out_buf, level_buf, sems):
    index, sections = lax.axis_index("sec"), lax.axis_size("sec")
    ends = (index == 0).astype(jnp.int32) + (index == sections - 1).astype(jnp.int32)
    present = 4.0 - ends.astype(f32)
    total = before_ref[...].astype(f32) + 2.0 * pooled_ref[...].astype(f32) + after_ref[...].astype(f32)
    level_buf[...] = (total / present).astype(bf16)
    copies = [pltpu.make_async_copy(level_buf, level_hbm, sems.at[PARTS])]
    copies[0].start()
    size = block_ref.shape[0] // PARTS
    for n in range(PARTS):
        rows = slice(n * size, (n + 1) * size)
        out_buf[rows] = (block_ref[rows] + late_ref[rows].astype(f32)).astype(bf16)
        copies.append(pltpu.make_async_copy(out_buf.at[rows], out_hbm.at[rows], sems.at[n]))
        copies[-1].start()
    for copy in copies:
        copy.wait()


PARTS = 4


def last(block, late, before, after, pooled):
    shapes = [jax.ShapeDtypeStruct(block.shape, bf16), jax.ShapeDtypeStruct(pooled.shape, bf16)]
    args = [pltpu.with_memory_space_constraint(x, pltpu.VMEM) for x in (block, late, before, after, pooled)]
    return pl.pallas_call(
        last_kernel,
        name="last",
        out_shape=shapes,
        in_specs=[vmem()] * 5,
        out_specs=[hbm()] * 2,
        scratch_shapes=[pltpu.VMEM(x.shape, x.dtype) for x in shapes] + [pltpu.SemaphoreType.DMA((PARTS + 1,))],
        compiler_params=pltpu.CompilerParams(vmem_limit_bytes=WORK_VMEM),
        cost_estimate=cost(1e6, 2e6),
    )(*args)


def call(kernel, name, out_shape, operands, mate=None, halves=False, work=(1e9, 4e6)):
    single = not isinstance(out_shape, list)
    edge = (out_shape if single else out_shape[0]).shape[1]
    scratch, far = [], []
    if mate is not None:
        scratch = [pltpu.VMEM((WIN, WIN), bf16), pltpu.SemaphoreType.DMA]
        far = [pltpu.with_memory_space_constraint(mate, pltpu.HBM)]
    if halves:
        scratch = [pltpu.VMEM((edge // 2 // LANE, edge, LANE), f32)]
    return pl.pallas_call(
        kernel,
        name=name,
        out_shape=out_shape,
        in_specs=[vmem()] * len(operands) + [hbm()] * len(far),
        out_specs=vmem() if single else [vmem()] * len(out_shape),
        scratch_shapes=scratch,
        compiler_params=pltpu.CompilerParams(vmem_limit_bytes=WORK_VMEM),
        cost_estimate=cost(*work),
    )(*[pltpu.with_memory_space_constraint(x, pltpu.VMEM) for x in operands], *far)


def two_row_device(
    tiles, row_taps, col_taps, row_starts, col_starts, feather_rows, feather_cols, footprint, offsets
):
    tile = tiles[0, 0]
    edge = row_starts.shape[3]
    devices = lax.axis_size("blk")

    def send(value, pairs):
        return lax.ppermute(value, "blk", pairs)

    def swap(pairs):
        return [(i, j) for i, j in pairs] + [(j, i) for i, j in pairs]

    in_chip = [(i, i ^ 1) for i in range(devices)]
    vertical_outer = swap([(0, 4), (3, 7)])
    vertical_inner = swap([(1, 5), (2, 6)])
    diagonal = swap([(1, 6), (2, 5)])
    across_inner = swap([(1, 2), (5, 6)])
    across_outer = swap([(0, 3), (4, 7)])
    outer_to_inner = [(0, 2), (3, 1), (4, 6), (7, 5)]

    asked, mine, aside, own_msg, near = prepare(
        row_taps[0, 0],
        col_taps[0, 0],
        row_starts.reshape(-1, 1, edge),
        col_starts.reshape(-1, 1, edge),
        footprint[0],
        offsets[0, 0].T,
        feather_rows[0],
        feather_cols[0],
        tile,
    )
    mate = send(tile, in_chip)
    outer = is_outer()
    got = send(asked, vertical_outer + diagonal)
    theirs = send(aside, in_chip)
    row = lax.broadcasted_iota(jnp.int32, mine.shape, 0)
    from_beside = jnp.logical_and(row >= BESIDE, row < BESIDE + 2)
    asking = jnp.where(from_beside, theirs, mine)
    down = send(jnp.where(outer, theirs, asking), across_outer + vertical_inner)

    block = jax.ShapeDtypeStruct((edge + EXTRA, edge), bf16)
    bare = jax.ShapeDtypeStruct((edge, edge), bf16)
    bare32 = jax.ShapeDtypeStruct((edge, edge), f32)
    pooled = jax.ShapeDtypeStruct((edge // 2, edge // 2), bf16)
    two = (4e9, 4e6)
    tiny = (1e4, 1e4)

    first = call(first_kernel, "first", block, (got, mine, theirs, near), mate, work=tiny)
    early = send(first, vertical_outer + across_inner)
    down, first = lax.optimization_barrier((down, first))
    second = call(second_kernel, "second", block, (down, mine, theirs, near), mate, work=two)
    own_msg, second = lax.optimization_barrier((own_msg, second))
    local = call(own_kernel, "own", bare32, (own_msg, mine, theirs, near), mate, work=two)
    second, local = lax.optimization_barrier((second, local))
    side = send(second, outer_to_inner)
    early, local = lax.optimization_barrier((early, local))
    late_out, pooled_out = call(
        merge_kernel, "merge", [bare, pooled], (second, early, got, down, mine, theirs), halves=True
    )
    pooled_late = send(pooled_out, vertical_inner)
    late = send(late_out, vertical_inner)
    block_so_far, pooled_all = call(
        blend_kernel,
        "blend",
        [bare32, pooled],
        (local, side, got, down, mine, theirs, early, pooled_late),
        halves=True,
        work=(5175000000.0, 1e6),
    )
    sections = lax.axis_size("sec")
    before = lax.ppermute(pooled_all, "sec", [(i, i + 1) for i in range(sections - 1)])
    after = lax.ppermute(pooled_all, "sec", [(i + 1, i) for i in range(sections - 1)])
    after, late = lax.optimization_barrier((after, late))
    blended, level = last(block_so_far, late, before, after, pooled_all)
    return blended[None, None], level[None, None]


def per_device(*args):
    if lax.axis_size("blk") == 2 * GY:
        return two_row_device(*args)
    return general_device(*args)


def solution(mesh):
    return jax.shard_map(
        per_device,
        mesh=mesh,
        in_specs=(
            P("sec", "blk", None, None),
            P("sec", "blk", None, None, None),
            P("sec", "blk", None, None, None),
            P("sec", "blk", None, None),
            P("sec", "blk", None, None),
            P("sec", "blk", None),
            P("sec", "blk", None),
            P("sec", "blk", None),
            P("sec", "blk", None, None),
        ),
        out_specs=(P("sec", "blk", None, None), P("sec", "blk", None, None)),
        check_vma=False,
    )
```
